512 devices in a mesh: dp: 32 (over z, core), ctx: 16 (over y, x).
Axes of the slice: x: 4, y: 4, z: 16, core: 2. Of those that a mesh axis runs over, the one named last changes fastest.
Arguments:
- features: bfloat16 [64, 1024, 768], P('dp', 'ctx'), may hold values from -75 to 75, as said below
- query_weight: bfloat16 [768, 256], replicated, may hold values from -0.21875 to 0.21875
- key_weight: bfloat16 [768, 256], replicated, may hold values from -0.21875 to 0.21875
- value_weight: bfloat16 [768, 768], replicated, may hold values from -0.21875 to 0.21875
- output_weight: bfloat16 [768, 768], replicated, may hold values from -0.875 to 0.875
- dilated_weight: bfloat16 [768, 1152], P('ctx'), may hold values from -0.125 to 0.125
- mixing_weight: bfloat16 [384, 768], replicated, may hold values from -0.3125 to 0.3125
- cotangent: bfloat16 [64, 1024, 768], P('dp', 'ctx'), may hold values from -0.0625 to 0.0625
Outputs:
- track_out: bfloat16 [64, 1024, 768], P('dp', 'ctx')
- dilated_grad: float32 [768, 1152], P('ctx')
The draws below stay inside these ranges and needn't reach their ends.
Inputs may be any that keep to these rules, and one draw needn't show every extreme that they name: `features`: Real-valued activations of varying scale over bins and channels.
All inputs are finite; a program needn't handle non-finite values.
Results may differ from the reference program's by a relative error of at most 0.019.
Values may be sent and summed in bfloat16 or wider, within the bound.
No kernel may reach another device: no remote copies, remote signals or barrier semaphores. Data moves between devices by JAX's collectives and lax.ppermute only.
A program may use at most 64 MiB of HBM per device.

```python
import math
import jax
import jax.numpy as jnp
from jax import lax

CHANNEL_COUNT = 768
F = 384
HEADS = 4
KEY = 64
VAL = 192
SEQUENCE_BINS = 1024
DILATION_BINS = 128
SEQUENCE_TOTAL = 64


def draw_features(key, part):
    key = jax.random.fold_in(key, 11)
    base_key, column_key, row_key = jax.random.split(key, 3)
    extent = (SEQUENCE_TOTAL, SEQUENCE_BINS, CHANNEL_COUNT)
    columns = jnp.exp(jax.random.uniform(column_key, (CHANNEL_COUNT,), jnp.float32, math.log(0.3), math.log(3.0)))
    rowwise = jnp.exp(jax.random.uniform(row_key, (SEQUENCE_TOTAL, SEQUENCE_BINS, 1), jnp.float32, math.log(0.5), math.log(5.0)))
    values = jax.random.truncated_normal(base_key, -4.0, 4.0, extent, jnp.float32)
    return (values * columns * rowwise).astype(jnp.bfloat16)


def level_of(own_key, dims, pieces, smallest, top_value):
    def one(axis_at, blocks):
        draws = jax.random.uniform(jax.random.fold_in(jax.random.fold_in(own_key, 6), axis_at), (blocks,), jnp.float32, smallest / len(pieces), top_value / len(pieces))
        return jnp.repeat(jnp.exp(draws), dims[axis_at] // blocks).reshape((-1,) + (1,) * (len(dims) - axis_at - 1))

    factor_of = one(*pieces[0])
    for cut in pieces[1:]:
        factor_of = factor_of * one(*cut)
    return factor_of


def normal_values(stream_key, dims, scale, bound, cuts=(), kind=jnp.bfloat16):
    entries = scale * jax.random.normal(stream_key, dims, jnp.float32)
    if cuts:
        entries = entries * level_of(stream_key, dims, cuts, -0.22, 0.18)
    return jnp.clip(entries, -bound, bound).astype(kind)


def setup_inputs(seed: int = 0) -> dict:
    streams_of = jax.random.split(jax.random.key(seed), 9)
    return {
        "features": draw_features(jax.random.fold_in(streams_of[8], 71), 0),
        "query_weight": normal_values(streams_of[1], (CHANNEL_COUNT, HEADS * KEY), CHANNEL_COUNT ** -0.5, 0.21875),
        "key_weight": normal_values(streams_of[2], (CHANNEL_COUNT, HEADS * KEY), CHANNEL_COUNT ** -0.5, 0.21875),
        "value_weight": normal_values(streams_of[3], (CHANNEL_COUNT, HEADS * VAL), CHANNEL_COUNT ** -0.5, 0.21875),
        "output_weight": normal_values(streams_of[4], (HEADS * VAL, CHANNEL_COUNT), (HEADS * VAL // 16) ** -0.5, 0.875),
        "dilated_weight": normal_values(streams_of[5], (CHANNEL_COUNT, 3 * F), (3 * CHANNEL_COUNT) ** -0.5, 0.125, ((0, 16),)),
        "mixing_weight": normal_values(streams_of[6], (F, CHANNEL_COUNT), F ** -0.5, 0.3125),
        "cotangent": normal_values(streams_of[7], (SEQUENCE_TOTAL, SEQUENCE_BINS, CHANNEL_COUNT), (1.0 / (SEQUENCE_TOTAL * SEQUENCE_BINS) ** 0.5), 0.0625, ((0, 32), (1, 16))),
    }


def layer_norm(values):
    center = values - lax.optimization_barrier(jnp.mean(values, axis=-1, keepdims=True))
    spread = lax.optimization_barrier(jnp.mean(center * center, axis=-1, keepdims=True))
    return center * lax.rsqrt(spread + 1e-05)

def head_norm(values, heads):
    shaped = values.reshape(values.shape[:-1] + (heads, values.shape[-1] // heads))
    shaped = shaped * lax.rsqrt(lax.optimization_barrier(jnp.mean(shaped * shaped, axis=-1, keepdims=True)) + 1e-06)
    return shaped.reshape(values.shape)

def gelu_exact(values):
    return jax.nn.gelu(values, approximate=False)

def gelu_slope(values):
    normal_cdf = 0.5 * (1.0 + lax.erf(values / math.sqrt(2.0)))
    normal_pdf = jnp.exp(-0.5 * values * values) / math.sqrt(2.0 * math.pi)
    return normal_cdf + values * normal_pdf

def reference(features, query_weight, key_weight, value_weight, output_weight, dilated_weight, mixing_weight, cotangent):

    def attend(sequence):
        normed = layer_norm(sequence.astype(jnp.float32)).astype(jnp.bfloat16)
        queries = head_norm(jnp.dot(normed, query_weight, preferred_element_type=jnp.float32), HEADS).astype(jnp.bfloat16)
        keys = head_norm(jnp.dot(normed, key_weight, preferred_element_type=jnp.float32), HEADS).astype(jnp.bfloat16)
        values = jnp.dot(normed, value_weight, preferred_element_type=jnp.float32).astype(jnp.bfloat16)
        query_heads = queries.astype(jnp.float32).reshape(SEQUENCE_BINS, HEADS, KEY)
        key_heads = keys.astype(jnp.float32).reshape(SEQUENCE_BINS, HEADS, KEY)
        value_heads = values.astype(jnp.float32).reshape(SEQUENCE_BINS, HEADS, VAL)
        scores = jnp.einsum('qhd,khd->hqk', query_heads, key_heads) * 0.25
        weights = jnp.exp(scores)
        total = lax.optimization_barrier(jnp.sum(weights, axis=-1))
        rounded = lax.optimization_barrier(weights.astype(jnp.bfloat16)).astype(jnp.float32)
        summed = jnp.einsum('hqk,khv->qhv', rounded, value_heads)
        mixed = (summed / jnp.transpose(total)[:, :, None]).astype(jnp.bfloat16).reshape(SEQUENCE_BINS, HEADS * VAL)
        attended = (sequence.astype(jnp.float32) + jnp.dot(mixed, output_weight, preferred_element_type=jnp.float32)).astype(jnp.bfloat16)
        raised_input = gelu_exact(layer_norm(attended.astype(jnp.float32))).astype(jnp.bfloat16)
        return (attended, raised_input)
    attended, raised_input = lax.map(attend, features)
    border_zeros = jnp.zeros((SEQUENCE_TOTAL, DILATION_BINS, CHANNEL_COUNT), raised_input.dtype)
    lower_neighbour = jnp.concatenate([border_zeros, raised_input[:, :SEQUENCE_BINS - DILATION_BINS]], axis=1).reshape(SEQUENCE_TOTAL * SEQUENCE_BINS, CHANNEL_COUNT)
    upper_neighbour = jnp.concatenate([raised_input[:, DILATION_BINS:], border_zeros], axis=1).reshape(SEQUENCE_TOTAL * SEQUENCE_BINS, CHANNEL_COUNT)
    middle = raised_input.reshape(SEQUENCE_TOTAL * SEQUENCE_BINS, CHANNEL_COUNT)
    hidden = jnp.dot(lower_neighbour, dilated_weight[:, :F], preferred_element_type=jnp.float32)
    hidden = hidden + jnp.dot(middle, dilated_weight[:, F:2 * F], preferred_element_type=jnp.float32)
    hidden = hidden + jnp.dot(upper_neighbour, dilated_weight[:, 2 * F:], preferred_element_type=jnp.float32)
    gated = gelu_exact(hidden).astype(jnp.bfloat16)
    attended_rows = attended.reshape(SEQUENCE_TOTAL * SEQUENCE_BINS, CHANNEL_COUNT).astype(jnp.float32)
    track_out = (attended_rows + jnp.dot(gated, mixing_weight, preferred_element_type=jnp.float32)).astype(jnp.bfloat16)
    back = jnp.dot(cotangent.reshape(SEQUENCE_TOTAL * SEQUENCE_BINS, CHANNEL_COUNT), jnp.transpose(mixing_weight), preferred_element_type=jnp.float32)
    slope = (back * gelu_slope(hidden)).astype(jnp.bfloat16)
    dilated_grad = jnp.concatenate([jnp.dot(jnp.transpose(lower_neighbour), slope, preferred_element_type=jnp.float32), jnp.dot(jnp.transpose(middle), slope, preferred_element_type=jnp.float32), jnp.dot(jnp.transpose(upper_neighbour), slope, preferred_element_type=jnp.float32)], axis=1)
    return (track_out.reshape(SEQUENCE_TOTAL, SEQUENCE_BINS, CHANNEL_COUNT), dilated_grad)
```

```python
import math

import jax
import jax.numpy as jnp
from jax import lax
from jax.sharding import PartitionSpec as P

HEADS = 4
NEAR = [[2 * (4 * far + near) + core for near in range(4)] for core in range(2) for far in range(4)]
FAR = [[2 * (4 * far + near) + core for far in range(4)] for core in range(2) for near in range(4)]


def from_behind(value, axis, steps):
    count = lax.axis_size(axis)
    initial, last = (max(0, -steps), min(count, count - steps))
    return lax.ppermute(value, axis, [(source, source + steps) for source in range(initial, last)])


def other_core(value):
    return lax.ppermute(value, "dp", [(source, source ^ 1) for source in range(32)])


def layer_norm(values):
    center = values - jnp.mean(values, axis=-1, keepdims=True)
    spread = jnp.mean(center * center, axis=-1, keepdims=True)
    return center * lax.rsqrt(spread + 1e-05)


def head_norm(values, heads):
    shaped = values.reshape(values.shape[:-1] + (heads, values.shape[-1] // heads))
    shaped = shaped * lax.rsqrt(jnp.mean(shaped * shaped, axis=-1, keepdims=True) + 1e-06)
    return shaped.reshape(values.shape)


def gelu_exact(values):
    return jax.nn.gelu(values, approximate=False)


def gelu_slope(values):
    normal_cdf = 0.5 * (1.0 + lax.erf(values / math.sqrt(2.0)))
    normal_pdf = jnp.exp(-0.5 * values * values) / math.sqrt(2.0 * math.pi)
    return normal_cdf + values * normal_pdf


def summed_over(value, groups):
    copies = jnp.broadcast_to(value[None], (4,) + value.shape)
    got = lax.all_to_all(copies, "dp", 0, 0, axis_index_groups=groups)
    return jnp.sum(got.astype(jnp.float32), axis=0).astype(jnp.bfloat16)


def shards(
    features,
    query_weight,
    key_weight,
    value_weight,
    output_weight,
    dilated_weight,
    mixing_weight,
    cotangent,
):
    f32, bf16 = jnp.float32, jnp.bfloat16
    complete_filters = lax.all_gather(dilated_weight, "ctx", axis=0, tiled=True)
    token_rows = features.reshape(128, 768)
    normed = layer_norm(token_rows.astype(f32)).astype(bf16)
    queries = head_norm(jnp.dot(normed, query_weight, preferred_element_type=f32), HEADS)
    queries = queries.astype(bf16)
    keys = head_norm(jnp.dot(normed, key_weight, preferred_element_type=f32), HEADS).astype(bf16)
    values = jnp.dot(normed, value_weight, preferred_element_type=f32).astype(bf16)
    q = queries.reshape(2, 2, 2, 16, 4, 64).transpose(0, 4, 1, 3, 2, 5).reshape(16, 16, 128)
    k = keys.reshape(2, 64, 4, 64).transpose(0, 2, 1, 3)
    v = values.reshape(2, 64, 4, 192).transpose(0, 2, 1, 3)
    kv = jnp.concatenate([k, v], axis=-1)
    kv = jnp.concatenate([kv[..., :128], kv[..., 128:]], axis=2)
    kv = jnp.broadcast_to(kv[:, :, None], (2, 4, 2, 128, 128)).reshape(16, 128, 128)
    got = lax.all_to_all(jnp.concatenate([kv, q], axis=1), "ctx", 0, 0)
    low, high = got[:, :64].reshape(1024, 128), got[:, 64:128].reshape(1024, 128)
    query = got[:, 128:].reshape(256, 128)
    query = jnp.concatenate([query[:, :64], query[:, 64:]], axis=0)
    key = low[:, :64]
    value = jnp.concatenate([low[:, 64:], high], axis=1)
    scores = 0.25 * lax.dot_general(
        query, key, (((1,), (1,)), ((), ())), preferred_element_type=f32
    )
    weights = jnp.exp(scores)
    total = jnp.sum(weights, axis=-1, keepdims=True)
    summed = jnp.dot(weights.astype(bf16), value, preferred_element_type=f32)
    mixed = (summed / total).astype(bf16)
    mixed = mixed.reshape(2, 16, 16, 192).transpose(1, 2, 0, 3).reshape(16, 16, 384)
    mixed = lax.all_to_all(mixed, "ctx", 0, 0)
    mixed = mixed.reshape(2, 4, 2, 16, 2, 192).transpose(0, 2, 4, 3, 1, 5).reshape(128, 768)
    attended = (
        token_rows.astype(f32) + jnp.dot(mixed, output_weight, preferred_element_type=f32)
    ).astype(bf16)
    raised_input = gelu_exact(layer_norm(attended.astype(f32))).astype(bf16)
    lifted_seq = raised_input.reshape(2, 64, 768)
    sources = (
        from_behind(lifted_seq, "ctx", 2).reshape(128, 768),
        raised_input,
        from_behind(lifted_seq, "ctx", -2).reshape(128, 768),
    )
    hidden = jnp.zeros((128, 384), f32)
    for tap in (1, 0, 2):
        hidden = hidden + jnp.dot(
            sources[tap],
            complete_filters[:, tap * 384 : (tap + 1) * 384],
            preferred_element_type=f32,
        )
    gated = gelu_exact(hidden).astype(bf16)
    track_out = (
        attended.astype(f32) + jnp.dot(gated, mixing_weight, preferred_element_type=f32)
    ).astype(bf16)
    back = lax.dot_general(
        cotangent.reshape(128, 768),
        mixing_weight,
        (((1,), (1,)), ((), ())),
        preferred_element_type=f32,
    )
    slope = (back * gelu_slope(hidden)).astype(bf16)
    core = lax.axis_index("dp") % 2
    parts = []
    for tap in range(3):
        parts.append(
            lax.dot_general(
                sources[tap], slope, (((0,), (0,)), ((), ())), preferred_element_type=f32
            )
        )
    grad = jnp.concatenate(parts, axis=1).astype(bf16).reshape(16, 2, 24, 1152)
    mine = lax.dynamic_index_in_dim(grad, core, 1, keepdims=False)
    theirs = lax.dynamic_index_in_dim(grad, 1 - core, 1, keepdims=False)
    grad = (mine.astype(f32) + other_core(theirs).astype(f32)).astype(bf16)
    grad = lax.all_to_all(grad, "ctx", 0, 0)
    grad = jnp.sum(grad.astype(f32), axis=0).astype(bf16)
    grad = summed_over(summed_over(grad, NEAR), FAR)
    rest = other_core(grad)
    first, second = jnp.where(core == 0, grad, rest), jnp.where(core == 0, rest, grad)
    dilated_grad = jnp.concatenate([first, second], axis=0).astype(f32)
    return (track_out.reshape(2, 64, 768), dilated_grad)


def solution(mesh):
    return jax.shard_map(
        shards,
        mesh=mesh,
        in_specs=(
            P("dp", "ctx", None),
            P(),
            P(),
            P(),
            P(),
            P("ctx", None),
            P(),
            P("dp", "ctx", None),
        ),
        out_specs=(P("dp", "ctx", None), P("ctx", None)),
        check_vma=False,
    )
```

```python
import math

import jax
import jax.numpy as jnp
import numpy as np
from jax import lax
from jax.experimental import pallas as pl
from jax.experimental.pallas import tpu as pltpu
from jax.sharding import PartitionSpec as P


NEAR = [[2 * (4 * far + near) + core for near in range(4)] for core in range(2) for far in range(4)]
FAR = [[2 * (4 * far + near) + core for far in range(4)] for core in range(2) for near in range(4)]
F32, BF16 = jnp.float32, jnp.bfloat16
PARAMS = pltpu.CompilerParams(vmem_limit_bytes=50 * 1024 * 1024)
VMEM = pl.BlockSpec(memory_space=pltpu.VMEM)
SMEM = pl.BlockSpec(memory_space=pltpu.SMEM)


def dot(a, b, dims=((1,), (0,))):
    return lax.dot_general(a, b, (dims, ((), ())), preferred_element_type=F32)


def moves(count, source):
    row = lax.broadcasted_iota(jnp.int32, (count, count), 0)
    column = lax.broadcasted_iota(jnp.int32, (count, count), 1)
    return jnp.where(source(row, column), 1.0, 0.0).astype(BF16)


def layer_norm(values):
    center = values - jnp.mean(values, axis=-1, keepdims=True)
    spread = jnp.mean(center * center, axis=-1, keepdims=True)
    return center * lax.rsqrt(spread + 1e-05)


def head_norm(values):
    row = lax.broadcasted_iota(jnp.int32, (256, 256), 0)
    column = lax.broadcasted_iota(jnp.int32, (256, 256), 1)
    same = jnp.where((row >> 6) == (column >> 6), 1.0 / 64.0, 0.0).astype(F32)
    mean = lax.dot_general(
        values * values,
        same,
        (((1,), (0,)), ((), ())),
        precision=lax.Precision.HIGHEST,
        preferred_element_type=F32,
    )
    return values * lax.rsqrt(mean + 1e-06)


def normal_cdf(values):
    return 0.5 * (1.0 + lax.erf(values * (1.0 / math.sqrt(2.0))))


def swap(tile):
    return pltpu.roll(tile, 64, 1)


def lower_lanes(rows):
    return lax.broadcasted_iota(jnp.int32, (rows, 128), 1) < 64


def front(core, x, wq, wk, wv, wd, mix, cot, message):
    own = x[...]
    normed = layer_norm(own.astype(F32)).astype(BF16)
    q = head_norm(dot(normed, wq[...]))
    k = head_norm(dot(normed, wk[...]))
    v = dot(normed, wv[...])
    to_queries = moves(128, lambda r, c: c == ((r >> 6) * 64 + ((r >> 1) & 15) * 4 + ((r >> 5) & 1) * 2 + (r & 1)))
    q = dot(to_queries, q.astype(BF16))
    low16, low64 = lower_lanes(16), lower_lanes(64)
    for s in range(2):
        rows = slice(64 * s, 64 * s + 64)
        for pair in range(2):
            key = k[rows, 128 * pair : 128 * pair + 128]
            left, middle, right = (v[rows, 384 * pair + 128 * t : 384 * pair + 128 * t + 128] for t in range(3))
            for odd in range(2):
                first = jnp.where(low64, swap(key) if odd else key, middle if odd else swap(middle))
                block = jnp.concatenate([first, right if odd else left], axis=0).astype(BF16)
                for half in range(2):
                    message[8 * s + 4 * pair + 2 * odd + half, 0:128, :] = block
            for half in range(2):
                start = 64 * s + 32 * half
                a = q[start : start + 16, 128 * pair : 128 * pair + 128]
                b = q[start + 16 : start + 32, 128 * pair : 128 * pair + 128]
                message[8 * s + 4 * pair + half, 128:144, :] = jnp.where(low16, a, swap(b)).astype(BF16)
                message[8 * s + 4 * pair + 2 + half, 128:144, :] = jnp.where(low16, swap(a), b).astype(BF16)
    to_bins = moves(128, lambda r, c: c == (((r >> 2) & 1) * 64 + (r >> 3) * 4 + (r & 3)))
    sent = dot(to_bins, own)
    back = dot(dot(to_bins, cot[...]).astype(BF16), mix[...], ((1,), (1,)))
    filters = wd[...].astype(F32)
    filters = jnp.where(core[0] == 0, filters[0:24], filters[24:48])
    for j in range(16):
        rows = slice(8 * j, 8 * j + 8)
        slab = jnp.concatenate([sent[rows], back[rows]], axis=1)
        slab = jnp.concatenate([slab, filters], axis=0).astype(BF16)
        for t in range(9):
            message[j, 144 + 32 * t : 176 + 32 * t, :] = slab[:, 128 * t : 128 * t + 128]


def attention(got, out, filters, sent):
    low = got[:, 0:64, :].reshape(1024, 128)
    high = got[:, 64:128, :].reshape(1024, 128)
    value = jnp.concatenate([low, high], axis=1)
    query = got[:, 128:144, :].reshape(256, 128)
    by_bins = moves(256, lambda r, c: c == (((r >> 1) & 15) * 16 + (r >> 5) * 2 + (r & 1)))
    query = dot(by_bins, query) * 0.25
    is_low = lower_lanes(256)
    queries = (jnp.where(is_low, query, 0.0).astype(BF16), jnp.where(is_low, swap(query), 0.0).astype(BF16))
    low16 = lower_lanes(16)
    for block in range(4):
        rows = queries[block // 2][128 * (block % 2) : 128 * (block % 2) + 128]
        weights = jnp.exp(dot(rows, low, ((1,), (1,))))
        total = jnp.sum(weights, axis=-1, keepdims=True)
        mixed = dot(weights.astype(BF16), value) / total
        for j in range(4):
            part = mixed[32 * j : 32 * j + 32]
            first = jnp.where(low16, swap(part[16:32, 0:128]), part[0:16, 0:128])
            out[4 * block + j] = jnp.concatenate([first, part[:, 128:256]], axis=0).astype(BF16)
    to_groups = moves(128, lambda r, c: c == (((r >> 1) & 15) * 8 + (r >> 5) * 2 + (r & 1)))
    for t in range(9):
        lanes = slice(128 * t, 128 * t + 128)
        pieces = [got[i, 144 + 32 * t : 176 + 32 * t, :].astype(F32) for i in range(16)]
        filters[:, lanes] = jnp.concatenate([p[8:32] for p in pieces], axis=0).astype(BF16)
        rows = jnp.concatenate([p[0:8] for p in pieces], axis=0).astype(BF16)
        sent[:, lanes] = dot(to_groups, rows).astype(BF16)


def middle(core, got, sent, wo, filters, others, order, attended, gated, mine, theirs):
    low16 = lower_lanes(16)
    tiles = []
    for pair in range(2):
        groups = [[], [], []]
        for s in range(2):
            for half in range(2):
                even, odd = (got[8 * s + 4 * pair + 2 * o + half].astype(F32) for o in range(2))
                e, o = even[0:16], odd[0:16]
                groups[0].append(even[16:48])
                groups[1] += [jnp.where(low16, swap(e), o), jnp.where(low16, e, swap(o))]
                groups[2].append(odd[16:48])
        tiles += [jnp.concatenate(g, axis=0) for g in groups]
    mixed = jnp.concatenate(tiles, axis=1).astype(BF16)
    result = (sent[:, 0:768].astype(F32) + dot(mixed, wo[...])).astype(BF16)
    attended[...] = result
    normed = layer_norm(result.astype(F32))
    lifted = (normed * normal_cdf(normed)).astype(BF16)
    lifted = dot(lifted, order[...])
    first, second = lifted[:, 0:384], lifted[:, 384:768]
    lifted = (
        jnp.where(core[0] == 0, first, second).astype(BF16),
        jnp.where(core[0] == 0, second, first).astype(BF16),
    )
    from_below = moves(128, lambda r, c: (c == r - 4) & ((r & 31) >= 4))
    from_above = moves(128, lambda r, c: (c == r + 4) & ((r & 31) < 28))
    weights = (filters, others)
    hidden = jnp.zeros((128, 384), F32)
    for part in range(2):
        below = dot(from_below, lifted[part]).astype(BF16)
        above = dot(from_above, lifted[part]).astype(BF16)
        for tap, rows in enumerate((below, lifted[part], above)):
            hidden = hidden + dot(rows, weights[part][:, 384 * tap : 384 * tap + 384])
    cdf = normal_cdf(hidden)
    gated[...] = (hidden * cdf).astype(BF16)
    pdf = jnp.exp(-0.5 * hidden * hidden) * (1.0 / math.sqrt(2.0 * math.pi))
    slope = (sent[:, 768:1152].astype(F32) * (cdf + hidden * pdf)).astype(BF16)
    slopes = (dot(from_above, slope).astype(BF16), slope, dot(from_below, slope).astype(BF16))
    for part, target in ((1, theirs), (0, mine)):
        for tap in range(3):
            target[:, 384 * tap : 384 * tap + 384] = dot(lifted[part], slopes[tap], ((0,), (0,))).astype(BF16)


def mixing(attended, gated, mix, track):
    result = (attended[...].astype(F32) + dot(gated[...], mix[...])).astype(BF16)
    by_block = moves(128, lambda r, c: c == (((r >> 1) & 3) * 32 + (r >> 3) * 2 + (r & 1)))
    track[...] = dot(by_block, result).astype(BF16)


def joined(mine, came, track, message):
    blank = jnp.zeros((8, 384), F32)
    for d in range(16):
        rows = slice(24 * d, 24 * d + 24)
        grad = mine[rows].astype(F32) + came[rows].astype(F32)
        top = jnp.concatenate([track[8 * d : 8 * d + 8].astype(F32), blank], axis=1)
        message[d] = jnp.concatenate([top, grad], axis=0).astype(BF16)


def summed(got, grad, track):
    total = got[0].astype(F32)
    rows = [total[0:8, 0:768]]
    for d in range(1, 16):
        block = got[d].astype(F32)
        rows.append(block[0:8, 0:768])
        total = total + block
    total = total[8:32].astype(BF16)
    for copy in range(4):
        grad[copy] = total
    natural = moves(128, lambda r, c: c == (((r >> 2) & 15) * 8 + (r >> 6) * 4 + (r & 3)))
    result = dot(natural, jnp.concatenate(rows, axis=0).astype(BF16))
    track[...] = result.astype(BF16)


def summed_again(got, grad):
    total = got[0].astype(F32) + got[1].astype(F32) + got[2].astype(F32) + got[3].astype(F32)
    total = total.astype(BF16)
    if len(grad.shape) == 3:
        for copy in range(grad.shape[0]):
            grad[copy] = total
    else:
        grad[...] = total


def call(kernel, outs, *args):
    return pl.pallas_call(
        kernel,
        out_shape=[jax.ShapeDtypeStruct(shape, BF16) for shape in outs],
        in_specs=[SMEM if a.dtype == jnp.int32 else VMEM for a in args],
        out_specs=[VMEM] * len(outs),
        compiler_params=PARAMS,
    )(*args)


def other_core(value):
    return lax.ppermute(value, "dp", [(source, source ^ 1) for source in range(32)])


def column_order():
    order = np.zeros((768, 768), np.float32)
    target = np.arange(768)
    order[(target % 384) // 24 * 48 + target // 384 * 24 + target % 24, target] = 1.0
    return jnp.asarray(order, BF16)


def shards(
    features,
    query_weight,
    key_weight,
    value_weight,
    output_weight,
    dilated_weight,
    mixing_weight,
    cotangent,
):
    core = lax.axis_index("dp") % 2
    flag = core.astype(jnp.int32).reshape(1)
    (message,) = call(
        front,
        [(16, 432, 128)],
        flag,
        features.reshape(128, 768),
        query_weight,
        key_weight,
        value_weight,
        dilated_weight,
        mixing_weight,
        cotangent.reshape(128, 768),
    )
    got = lax.all_to_all(message, "ctx", 0, 0)
    mixed, filters, sent = call(attention, [(16, 48, 128), (384, 1152), (128, 1152)], got)
    others = other_core(filters)
    got = lax.all_to_all(mixed, "ctx", 0, 0)
    attended, gated, mine, theirs = call(
        middle,
        [(128, 768), (128, 384), (384, 1152), (384, 1152)],
        flag,
        got,
        sent,
        output_weight,
        filters,
        others,
        column_order(),
    )
    came = other_core(theirs)
    (track,) = call(mixing, [(128, 768)], attended, gated, mixing_weight)
    (message,) = call(joined, [(16, 32, 1152)], mine, came, track)
    got = lax.all_to_all(message, "ctx", 0, 0)
    grad, track = call(summed, [(4, 24, 1152), (128, 768)], got)
    got = lax.all_to_all(grad, "dp", 0, 0, axis_index_groups=NEAR)
    (grad,) = call(summed_again, [(4, 24, 1152)], got)
    got = lax.all_to_all(grad, "dp", 0, 0, axis_index_groups=FAR)
    (grad,) = call(summed_again, [(24, 1152)], got)
    rest = other_core(grad)
    first, second = jnp.where(core == 0, grad, rest), jnp.where(core == 0, rest, grad)
    dilated_grad = jnp.concatenate([first, second], axis=0).astype(F32)
    return (track.reshape(2, 64, 768), dilated_grad)


def solution(mesh):
    return jax.shard_map(
        shards,
        mesh=mesh,
        in_specs=(
            P("dp", "ctx", None),
            P(),
            P(),
            P(),
            P(),
            P("ctx", None),
            P(),
            P("dp", "ctx", None),
        ),
        out_specs=(P("dp", "ctx", None), P("ctx", None)),
        check_vma=False,
    )
```

```python
import math

import jax
import jax.numpy as jnp
import numpy as np
from jax import lax
from jax.experimental import pallas as pl
from jax.experimental.pallas import tpu as pltpu
from jax.sharding import PartitionSpec as P


NEAR = [[2 * (4 * far + near) + core for near in range(4)] for core in range(2) for far in range(4)]
FAR = [[2 * (4 * far + near) + core for far in range(4)] for core in range(2) for near in range(4)]
CLOSE = [[8 * far + member for member in range(8)] for far in range(4)]
F32, BF16 = jnp.float32, jnp.bfloat16
VMEM = pl.BlockSpec(memory_space=pltpu.VMEM)
SMEM = pl.BlockSpec(memory_space=pltpu.SMEM)


def dot(a, b, dims=((1,), (0,))):
    return lax.dot_general(a, b, (dims, ((), ())), preferred_element_type=F32)


def moves(count, source):
    row = lax.broadcasted_iota(jnp.int32, (count, count), 0)
    column = lax.broadcasted_iota(jnp.int32, (count, count), 1)
    return jnp.where(source(row, column), 1.0, 0.0).astype(BF16)


def layer_norm(values):
    center = values - jnp.mean(values, axis=-1, keepdims=True)
    spread = jnp.mean(center * center, axis=-1, keepdims=True)
    return center * lax.rsqrt(spread + 1e-05)


def head_norm(values):
    row = lax.broadcasted_iota(jnp.int32, (256, 256), 0)
    column = lax.broadcasted_iota(jnp.int32, (256, 256), 1)
    same = jnp.where((row >> 6) == (column >> 6), 1.0 / 64.0, 0.0).astype(F32)
    mean = lax.dot_general(
        values * values,
        same,
        (((1,), (0,)), ((), ())),
        precision=lax.Precision.HIGHEST,
        preferred_element_type=F32,
    )
    return values * lax.rsqrt(mean + 1e-06)


def normal_cdf(values):
    return 0.5 * (1.0 + lax.erf(values * (1.0 / math.sqrt(2.0))))


def swap(tile):
    return pltpu.roll(tile, 64, 1)


def lower_lanes(rows):
    return lax.broadcasted_iota(jnp.int32, (rows, 128), 1) < 64


def fetch(pieces, semaphores):
    copies = [pltpu.make_async_copy(a, b, semaphores.at[n]) for n, (a, b) in enumerate(pieces)]
    for copy in copies:
        copy.start()
    return copies


def front(core, x, wd, cot, mix, wq, wk, wv, message, carry, x_here, wd_here, cot_here, mix_here, wq_here, wk_here, wv_here, semaphores):
    pieces = [(x, x_here), (wd, wd_here), (cot, cot_here)]
    for weight, here in ((wq, wq_here), (wk, wk_here), (mix, mix_here), (wv, wv_here)):
        step = weight.shape[0] // 4
        pieces += [(weight.at[pl.ds(step * n, step)], here.at[pl.ds(step * n, step)]) for n in range(4)]
    copies = fetch(pieces, semaphores)
    to_queries = moves(128, lambda r, c: c == ((r >> 6) * 64 + ((r >> 1) & 15) * 4 + ((r >> 5) & 1) * 2 + (r & 1)))
    to_bins = moves(128, lambda r, c: c == (((r >> 2) & 1) * 64 + (r >> 3) * 4 + (r & 3)))
    copies[0].wait()
    normed = layer_norm(x_here[...].astype(F32)).astype(BF16)
    sent = dot(to_bins, x_here[...])
    copies[1].wait()
    filters = wd_here[...].astype(F32)
    filters = jnp.where(core[0] == 0, filters[0:24], filters[24:48]).astype(BF16)
    for t in range(9):
        tile = filters[:, 128 * t : 128 * t + 128]
        for j in range(16):
            message[j, 144 + 24 * t : 168 + 24 * t, :] = tile
    for copy in copies[2:7]:
        copy.wait()
    moved = dot(to_bins, cot_here[...]).astype(BF16)
    q = head_norm(dot(normed, wq_here[...]))
    q = dot(to_queries, q.astype(BF16))
    for copy in copies[7:11]:
        copy.wait()
    k = head_norm(dot(normed, wk_here[...]))
    for copy in copies[11:15]:
        copy.wait()
    back = dot(moved, mix_here[...], ((1,), (1,)))
    for j in range(16):
        rows = slice(8 * j, 8 * j + 8)
        carry[j] = jnp.concatenate([sent[rows], back[rows]], axis=1).astype(BF16)
    for copy in copies[15:19]:
        copy.wait()
    v = dot(normed, wv_here[...])
    low16, low64 = lower_lanes(16), lower_lanes(64)
    for s in range(2):
        rows = slice(64 * s, 64 * s + 64)
        for pair in range(2):
            key = k[rows, 128 * pair : 128 * pair + 128]
            left, middle, right = (v[rows, 384 * pair + 128 * t : 384 * pair + 128 * t + 128] for t in range(3))
            for odd in range(2):
                first = jnp.where(low64, swap(key) if odd else key, middle if odd else swap(middle))
                block = jnp.concatenate([first, right if odd else left], axis=0).astype(BF16)
                for half in range(2):
                    message[8 * s + 4 * pair + 2 * odd + half, 0:128, :] = block
            for half in range(2):
                start = 64 * s + 32 * half
                a = q[start : start + 16, 128 * pair : 128 * pair + 128]
                b = q[start + 16 : start + 32, 128 * pair : 128 * pair + 128]
                message[8 * s + 4 * pair + half, 128:144, :] = jnp.where(low16, a, swap(b)).astype(BF16)
                message[8 * s + 4 * pair + 2 + half, 128:144, :] = jnp.where(low16, swap(a), b).astype(BF16)


def attention(got, carry, out, filters):
    low = got[:, 0:64, :].reshape(1024, 128)
    high = got[:, 64:128, :].reshape(1024, 128)
    value = jnp.concatenate([low, high], axis=1)
    query = got[:, 128:144, :].reshape(256, 128)
    by_bins = moves(256, lambda r, c: c == (((r >> 1) & 15) * 16 + (r >> 5) * 2 + (r & 1)))
    query = dot(by_bins, query) * 0.25
    is_low = lower_lanes(256)
    queries = (jnp.where(is_low, query, 0.0).astype(BF16), jnp.where(is_low, swap(query), 0.0).astype(BF16))
    low16 = lower_lanes(16)
    for block in range(4):
        rows = queries[block // 2][128 * (block % 2) : 128 * (block % 2) + 128]
        weights = jnp.exp(dot(rows, low, ((1,), (1,))))
        total = jnp.sum(weights, axis=-1, keepdims=True)
        mixed = dot(weights.astype(BF16), value) / total
        for j in range(4):
            part = mixed[32 * j : 32 * j + 32]
            first = jnp.where(low16, swap(part[16:32, 0:128]), part[0:16, 0:128])
            out[4 * block + j, 0:48, :] = jnp.concatenate([first, part[:, 128:256]], axis=0).astype(BF16)
    for t in range(9):
        lanes = slice(128 * t, 128 * t + 128)
        pieces = [got[i, 144 + 24 * t : 168 + 24 * t, :].astype(F32) for i in range(16)]
        filters[:, lanes] = jnp.concatenate(pieces, axis=0).astype(BF16)
        for j in range(16):
            out[j, 48 + 8 * t : 56 + 8 * t, :] = carry[j, :, lanes]


def middle(core, got, wo, filters, others, order, attended, gated, mine, theirs):
    to_groups = moves(128, lambda r, c: c == (((r >> 1) & 15) * 8 + (r >> 5) * 2 + (r & 1)))
    sent = []
    for t in range(9):
        rows = [got[i, 48 + 8 * t : 56 + 8 * t, :].astype(F32) for i in range(16)]
        sent.append(jnp.concatenate(rows, axis=0).astype(BF16))
    sent = dot(to_groups, jnp.concatenate(sent, axis=1))
    low16 = lower_lanes(16)
    tiles = []
    for pair in range(2):
        groups = [[], [], []]
        for s in range(2):
            for half in range(2):
                even, odd = (got[8 * s + 4 * pair + 2 * o + half, 0:48, :].astype(F32) for o in range(2))
                e, o = even[0:16], odd[0:16]
                groups[0].append(even[16:48])
                groups[1] += [jnp.where(low16, swap(e), o), jnp.where(low16, e, swap(o))]
                groups[2].append(odd[16:48])
        tiles += [jnp.concatenate(g, axis=0) for g in groups]
    mixed = jnp.concatenate(tiles, axis=1).astype(BF16)
    result = (sent[:, 0:768] + dot(mixed, wo[...])).astype(BF16)
    attended[...] = result
    normed = layer_norm(result.astype(F32))
    lifted = (normed * normal_cdf(normed)).astype(BF16)
    lifted = dot(lifted, order[...])
    first, second = lifted[:, 0:384], lifted[:, 384:768]
    lifted = (
        jnp.where(core[0] == 0, first, second).astype(BF16),
        jnp.where(core[0] == 0, second, first).astype(BF16),
    )
    from_below = moves(128, lambda r, c: (c == r - 4) & ((r & 31) >= 4))
    from_above = moves(128, lambda r, c: (c == r + 4) & ((r & 31) < 28))
    weights = (filters, others)
    hidden = jnp.zeros((128, 384), F32)
    for part in range(2):
        below = dot(from_below, lifted[part]).astype(BF16)
        above = dot(from_above, lifted[part]).astype(BF16)
        for tap, rows in enumerate((below, lifted[part], above)):
            hidden = hidden + dot(rows, weights[part][:, 384 * tap : 384 * tap + 384])
    cdf = normal_cdf(hidden)
    gated[...] = (hidden * cdf).astype(BF16)
    pdf = jnp.exp(-0.5 * hidden * hidden) * (1.0 / math.sqrt(2.0 * math.pi))
    slope = (sent[:, 768:1152] * (cdf + hidden * pdf)).astype(BF16)
    slopes = (dot(from_above, slope).astype(BF16), slope, dot(from_below, slope).astype(BF16))
    for part, target in ((1, theirs), (0, mine)):
        for tap in range(3):
            grad = dot(lifted[part], slopes[tap], ((0,), (0,)))
            for d in range(16):
                for t in range(3):
                    start = 24 * (3 * tap + t)
                    tile = grad[24 * d : 24 * d + 24, 128 * t : 128 * t + 128]
                    target[d, start : start + 24, :] = tile.astype(BF16)


def mixing(attended, gated, mix, track):
    result = (attended[...].astype(F32) + dot(gated[...], mix[...])).astype(BF16)
    by_block = moves(128, lambda r, c: c == (((r >> 1) & 3) * 32 + (r >> 3) * 2 + (r & 1)))
    track[...] = dot(by_block, result).astype(BF16)


def joined(mine, came, track, message):
    for d in range(16):
        for t in range(6):
            message[d, 8 * t : 8 * t + 8, :] = track[8 * d : 8 * d + 8, 128 * t : 128 * t + 128]
        message[d, 48:264, :] = (mine[d].astype(F32) + came[d].astype(F32)).astype(BF16)


def summed(got, grad, track):
    total = got[0, 48:264, :].astype(F32)
    for d in range(1, 16):
        total = total + got[d, 48:264, :].astype(F32)
    total = jnp.concatenate([total, jnp.zeros((8, 128), F32)], axis=0)
    for near in range(4):
        grad[near] = total[56 * near : 56 * near + 56].astype(BF16)
    natural = moves(128, lambda r, c: c == (((r >> 2) & 15) * 8 + (r >> 6) * 4 + (r & 3)))
    for t in range(6):
        rows = [got[d, 8 * t : 8 * t + 8, :].astype(F32) for d in range(16)]
        rows = dot(natural, jnp.concatenate(rows, axis=0).astype(BF16))
        track[:, 128 * t : 128 * t + 128] = rows.astype(BF16)


def summed_again(got, grad):
    total = got[0].astype(F32) + got[1].astype(F32) + got[2].astype(F32) + got[3].astype(F32)
    total = total.astype(BF16)
    for copy in range(grad.shape[0]):
        grad[copy] = total


def ordered(got, grad):
    for core in range(2):
        rows = jnp.concatenate([got[2 * near + core].astype(F32) for near in range(4)], axis=0)
        for t in range(9):
            grad[24 * core : 24 * core + 24, 128 * t : 128 * t + 128] = rows[24 * t : 24 * t + 24]


def call(kernel, outs, *args, dtype=BF16, fetched=()):
    scratch = [pltpu.VMEM(shape, BF16) for shape in fetched]
    if fetched:
        scratch.append(pltpu.SemaphoreType.DMA((19,)))
    return pl.pallas_call(
        kernel,
        out_shape=[jax.ShapeDtypeStruct(shape, dtype) for shape in outs],
        in_specs=[
            SMEM if a.dtype == jnp.int32 else pl.BlockSpec(memory_space=pl.ANY) if fetched else VMEM
            for a in args
        ],
        out_specs=[VMEM] * len(outs),
        scratch_shapes=scratch,
        compiler_params=pltpu.CompilerParams(vmem_limit_bytes=(56 if fetched else 32) * 1024 * 1024),
    )(*args)


def other_core(value):
    return lax.ppermute(value, "dp", [(source, source ^ 1) for source in range(32)])


def column_order():
    order = np.zeros((768, 768), np.float32)
    target = np.arange(768)
    order[(target % 384) // 24 * 48 + target // 384 * 24 + target % 24, target] = 1.0
    return jnp.asarray(order, BF16)


def shards(
    features,
    query_weight,
    key_weight,
    value_weight,
    output_weight,
    dilated_weight,
    mixing_weight,
    cotangent,
):
    core = lax.axis_index("dp") % 2
    flag = core.astype(jnp.int32).reshape(1)
    message, carry = call(
        front,
        [(16, 360, 128), (16, 8, 1152)],
        flag,
        features.reshape(128, 768),
        dilated_weight,
        cotangent.reshape(128, 768),
        mixing_weight,
        query_weight,
        key_weight,
        value_weight,
        fetched=((128, 768), (48, 1152), (128, 768), (384, 768), (768, 256), (768, 256), (768, 768)),
    )
    got = lax.all_to_all(message, "ctx", 0, 0)
    mixed, filters = call(attention, [(16, 120, 128), (384, 1152)], got, carry)
    others = other_core(filters)
    got = lax.all_to_all(mixed, "ctx", 0, 0)
    attended, gated, mine, theirs = call(
        middle,
        [(128, 768), (128, 384), (16, 216, 128), (16, 216, 128)],
        flag,
        got,
        output_weight,
        filters,
        others,
        column_order(),
    )
    came = other_core(theirs)
    (track,) = call(mixing, [(128, 768)], attended, gated, mixing_weight)
    (message,) = call(joined, [(16, 264, 128)], mine, came, track)
    got = lax.all_to_all(message, "ctx", 0, 0)
    grad, track = call(summed, [(4, 56, 128), (128, 768)], got)
    got = lax.all_to_all(grad, "dp", 0, 0, axis_index_groups=NEAR)
    (grad,) = call(summed_again, [(4, 56, 128)], got)
    got = lax.all_to_all(grad, "dp", 0, 0, axis_index_groups=FAR)
    (grad,) = call(summed_again, [(8, 56, 128)], got)
    got = lax.all_to_all(grad, "dp", 0, 0, axis_index_groups=CLOSE)
    (dilated_grad,) = call(ordered, [(48, 1152)], got, dtype=F32)
    return (track.reshape(2, 64, 768), dilated_grad)


def solution(mesh):
    return jax.shard_map(
        shards,
        mesh=mesh,
        in_specs=(
            P("dp", "ctx", None),
            P(),
            P(),
            P(),
            P(),
            P("ctx", None),
            P(),
            P("dp", "ctx", None),
        ),
        out_specs=(P("dp", "ctx", None), P("ctx", None)),
        check_vma=False,
    )
```

```python
import math

import jax
import jax.numpy as jnp
import numpy as np
from jax import lax
from jax.experimental import pallas as pl
from jax.experimental.pallas import tpu as pltpu
from jax.sharding import PartitionSpec as P


NEAR = [[2 * (4 * far + near) + core for near in range(4)] for core in range(2) for far in range(4)]
FAR = [[2 * (4 * far + near) + core for far in range(4)] for core in range(2) for near in range(4)]
CLOSE = [[4 * pair + member for member in range(4)] for pair in range(8)]
F32, BF16 = jnp.float32, jnp.bfloat16
VMEM = pl.BlockSpec(memory_space=pltpu.VMEM)
SMEM = pl.BlockSpec(memory_space=pltpu.SMEM)


def dot(a, b, dims=((1,), (0,))):
    return lax.dot_general(a, b, (dims, ((), ())), preferred_element_type=F32)


def moves(count, source):
    row = lax.broadcasted_iota(jnp.int32, (count, count), 0)
    column = lax.broadcasted_iota(jnp.int32, (count, count), 1)
    return jnp.where(source(row, column), 1.0, 0.0).astype(BF16)


def layer_norm(values):
    center = values - jnp.mean(values, axis=-1, keepdims=True)
    spread = jnp.mean(center * center, axis=-1, keepdims=True)
    return center * lax.rsqrt(spread + 1e-05)


def head_norm(values):
    row = lax.broadcasted_iota(jnp.int32, (256, 256), 0)
    column = lax.broadcasted_iota(jnp.int32, (256, 256), 1)
    same = jnp.where((row >> 6) == (column >> 6), 1.0 / 64.0, 0.0).astype(BF16)
    square = values * values
    high = square.astype(BF16)
    mean = dot(high, same) + dot((square - high.astype(F32)).astype(BF16), same)
    return values * lax.rsqrt(mean + 1e-06)


def normal_cdf(values):
    return 0.5 * (1.0 + lax.erf(values * (1.0 / math.sqrt(2.0))))


def swap(tile):
    return pltpu.roll(tile, 64, 1)


def lower_lanes(rows):
    return lax.broadcasted_iota(jnp.int32, (rows, 128), 1) < 64


def fetch(pieces, semaphores):
    copies = [pltpu.make_async_copy(a, b, semaphores.at[n]) for n, (a, b) in enumerate(pieces)]
    for copy in copies:
        copy.start()
    return copies


def front(core, x, wd, wq, wk, wv, message, x_here, wd_here, wq_here, wk_here, wv_here, semaphores):
    pieces = [(x, x_here), (wd, wd_here)]
    for weight, here in ((wq, wq_here), (wk, wk_here), (wv, wv_here)):
        step = weight.shape[0] // 2
        pieces += [(weight.at[pl.ds(step * n, step)], here.at[pl.ds(step * n, step)]) for n in range(2)]
    copies = fetch(pieces, semaphores)
    to_queries = moves(128, lambda r, c: c == ((r >> 6) * 64 + ((r >> 1) & 15) * 4 + ((r >> 5) & 1) * 2 + (r & 1)))
    copies[0].wait()
    normed = layer_norm(x_here[...].astype(F32)).astype(BF16)
    copies[1].wait()
    filters = wd_here[...].astype(F32)
    filters = jnp.where(core[0] == 0, filters[0:24], filters[24:48]).astype(BF16)
    for t in range(9):
        tile = filters[:, 128 * t : 128 * t + 128]
        for j in range(16):
            message[j, 144 + 24 * t : 168 + 24 * t, :] = tile
    for copy in copies[2:4]:
        copy.wait()
    q = head_norm(dot(normed, wq_here[...]))
    q = dot(to_queries, q.astype(BF16))
    for copy in copies[4:6]:
        copy.wait()
    k = head_norm(dot(normed, wk_here[...]))
    for copy in copies[6:8]:
        copy.wait()
    v = dot(normed, wv_here[...])
    low16, low64 = lower_lanes(16), lower_lanes(64)
    for s in range(2):
        rows = slice(64 * s, 64 * s + 64)
        for pair in range(2):
            key = k[rows, 128 * pair : 128 * pair + 128]
            left, middle, right = (v[rows, 384 * pair + 128 * t : 384 * pair + 128 * t + 128] for t in range(3))
            for odd in range(2):
                first = jnp.where(low64, swap(key) if odd else key, middle if odd else swap(middle))
                block = jnp.concatenate([first, right if odd else left], axis=0).astype(BF16)
                for half in range(2):
                    message[8 * s + 4 * pair + 2 * odd + half, 0:128, :] = block
            for half in range(2):
                start = 64 * s + 32 * half
                a = q[start : start + 16, 128 * pair : 128 * pair + 128]
                b = q[start + 16 : start + 32, 128 * pair : 128 * pair + 128]
                message[8 * s + 4 * pair + half, 128:144, :] = jnp.where(low16, a, swap(b)).astype(BF16)
                message[8 * s + 4 * pair + 2 + half, 128:144, :] = jnp.where(low16, swap(a), b).astype(BF16)


def attention(got, x, cot, mix, out, filters):
    low = got[:, 0:64, :].reshape(1024, 128)
    high = got[:, 64:128, :].reshape(1024, 128)
    value = jnp.concatenate([low, high], axis=1)
    query = got[:, 128:144, :].reshape(256, 128)
    by_bins = moves(256, lambda r, c: c == (((r >> 1) & 15) * 16 + (r >> 5) * 2 + (r & 1)))
    query = dot(by_bins, query) * 0.25
    is_low = lower_lanes(256)
    queries = (jnp.where(is_low, query, 0.0).astype(BF16), jnp.where(is_low, swap(query), 0.0).astype(BF16))
    low16 = lower_lanes(16)
    for block in range(4):
        rows = queries[block // 2][128 * (block % 2) : 128 * (block % 2) + 128]
        weights = jnp.exp(dot(rows, low, ((1,), (1,))))
        total = jnp.sum(weights, axis=-1, keepdims=True)
        mixed = dot(weights.astype(BF16), value) / total
        for j in range(4):
            part = mixed[32 * j : 32 * j + 32]
            first = jnp.where(low16, swap(part[16:32, 0:128]), part[0:16, 0:128])
            out[4 * block + j, 0:48, :] = jnp.concatenate([first, part[:, 128:256]], axis=0).astype(BF16)
    for t in range(9):
        lanes = slice(128 * t, 128 * t + 128)
        pieces = [got[i, 144 + 24 * t : 168 + 24 * t, :].astype(F32) for i in range(16)]
        filters[:, lanes] = jnp.concatenate(pieces, axis=0).astype(BF16)
    to_bins = moves(128, lambda r, c: c == (((r >> 2) & 1) * 64 + (r >> 3) * 4 + (r & 3)))
    sent = dot(to_bins, x[...]).astype(BF16)
    back = dot(dot(to_bins, cot[...]).astype(BF16), mix[...], ((1,), (1,))).astype(BF16)
    for t in range(9):
        rows = sent[:, 128 * t : 128 * t + 128] if t < 6 else back[:, 128 * t - 768 : 128 * t - 640]
        for j in range(16):
            out[j, 48 + 8 * t : 56 + 8 * t, :] = rows[8 * j : 8 * j + 8]


def middle(core, got, wo, filters, others, order, attended, gated, own, slopes, theirs):
    to_groups = moves(128, lambda r, c: c == (((r >> 1) & 15) * 8 + (r >> 5) * 2 + (r & 1)))
    sent = []
    for t in range(9):
        rows = [got[i, 48 + 8 * t : 56 + 8 * t, :].astype(F32) for i in range(16)]
        sent.append(jnp.concatenate(rows, axis=0).astype(BF16))
    sent = dot(to_groups, jnp.concatenate(sent, axis=1))
    low16 = lower_lanes(16)
    tiles = []
    for pair in range(2):
        groups = [[], [], []]
        for s in range(2):
            for half in range(2):
                even, odd = (got[8 * s + 4 * pair + 2 * o + half, 0:48, :].astype(F32) for o in range(2))
                e, o = even[0:16], odd[0:16]
                groups[0].append(even[16:48])
                groups[1] += [jnp.where(low16, swap(e), o), jnp.where(low16, e, swap(o))]
                groups[2].append(odd[16:48])
        tiles += [jnp.concatenate(g, axis=0) for g in groups]
    mixed = jnp.concatenate(tiles, axis=1).astype(BF16)
    result = (sent[:, 0:768] + dot(mixed, wo[...])).astype(BF16)
    attended[...] = result
    normed = layer_norm(result.astype(F32))
    lifted = (normed * normal_cdf(normed)).astype(BF16)
    lifted = dot(lifted, order[...])
    first, second = lifted[:, 0:384], lifted[:, 384:768]
    lifted = (
        jnp.where(core[0] == 0, first, second).astype(BF16),
        jnp.where(core[0] == 0, second, first).astype(BF16),
    )
    from_below = moves(128, lambda r, c: (c == r - 4) & ((r & 31) >= 4))
    from_above = moves(128, lambda r, c: (c == r + 4) & ((r & 31) < 28))
    weights = (filters, others)
    hidden = jnp.zeros((128, 384), F32)
    for part in range(2):
        below = dot(from_below, lifted[part]).astype(BF16)
        above = dot(from_above, lifted[part]).astype(BF16)
        for tap, rows in enumerate((below, lifted[part], above)):
            hidden = hidden + dot(rows, weights[part][:, 384 * tap : 384 * tap + 384])
    cdf = normal_cdf(hidden)
    gated[...] = (hidden * cdf).astype(BF16)
    pdf = jnp.exp(-0.5 * hidden * hidden) * (1.0 / math.sqrt(2.0 * math.pi))
    slope = (sent[:, 768:1152] * (cdf + hidden * pdf)).astype(BF16)
    own[...] = lifted[0]
    slopes[:, 0:384] = dot(from_above, slope).astype(BF16)
    slopes[:, 384:768] = slope
    slopes[:, 768:1152] = dot(from_below, slope).astype(BF16)
    gradient(lifted[1], slopes, theirs)


def gradient(lifted, slopes, target):
    for tap in range(3):
        grad = dot(lifted, slopes[:, 384 * tap : 384 * tap + 384], ((0,), (0,)))
        for d in range(16):
            for t in range(3):
                start = 24 * (3 * tap + t)
                tile = grad[24 * d : 24 * d + 24, 128 * t : 128 * t + 128]
                target[d, start : start + 24, :] = tile.astype(BF16)


def rest(attended, gated, mix, lifted, slopes, track, mine):
    result = (attended[...].astype(F32) + dot(gated[...], mix[...])).astype(BF16)
    by_block = moves(128, lambda r, c: c == (((r >> 1) & 3) * 32 + (r >> 3) * 2 + (r & 1)))
    track[...] = dot(by_block, result).astype(BF16)
    gradient(lifted[...], slopes, mine)


def joined(mine, came, track, message):
    for d in range(16):
        for t in range(6):
            message[d, 8 * t : 8 * t + 8, :] = track[8 * d : 8 * d + 8, 128 * t : 128 * t + 128]
        message[d, 48:264, :] = (mine[d].astype(F32) + came[d].astype(F32)).astype(BF16)


def summed(got, grad, track):
    total = got[0, 48:264, :].astype(F32)
    for d in range(1, 16):
        total = total + got[d, 48:264, :].astype(F32)
    total = jnp.concatenate([total, jnp.zeros((8, 128), F32)], axis=0)
    for near in range(4):
        half = 112 * (near % 2)
        grad[near] = total[half : half + 112].astype(BF16)
    natural = moves(128, lambda r, c: c == (((r >> 2) & 15) * 8 + (r >> 6) * 4 + (r & 3)))
    for t in range(6):
        rows = [got[d, 8 * t : 8 * t + 8, :].astype(F32) for d in range(16)]
        rows = dot(natural, jnp.concatenate(rows, axis=0).astype(BF16))
        track[:, 128 * t : 128 * t + 128] = rows.astype(BF16)


def summed_again(got, grad):
    total = got[0].astype(F32) + got[1].astype(F32) + got[2].astype(F32) + got[3].astype(F32)
    total = total.astype(BF16)
    for copy in range(grad.shape[0]):
        grad[copy] = total


def ordered(got, grad):
    for core in range(2):
        rows = jnp.concatenate([got[2 * half + core].astype(F32) for half in range(2)], axis=0)
        for t in range(9):
            grad[24 * core : 24 * core + 24, 128 * t : 128 * t + 128] = rows[24 * t : 24 * t + 24]


def call(kernel, outs, *args, dtype=BF16, fetched=()):
    scratch = [pltpu.VMEM(shape, BF16) for shape in fetched]
    if fetched:
        scratch.append(pltpu.SemaphoreType.DMA((8,)))
    return pl.pallas_call(
        kernel,
        out_shape=[jax.ShapeDtypeStruct(shape, dtype) for shape in outs],
        in_specs=[
            SMEM if a.dtype == jnp.int32 else pl.BlockSpec(memory_space=pl.ANY) if fetched else VMEM
            for a in args
        ],
        out_specs=[VMEM] * len(outs),
        scratch_shapes=scratch,
        compiler_params=pltpu.CompilerParams(vmem_limit_bytes=(56 if fetched else 32) * 1024 * 1024),
    )(*args)


def other_core(value):
    return lax.ppermute(value, "dp", [(source, source ^ 1) for source in range(32)])


def column_order():
    order = np.zeros((768, 768), np.float32)
    target = np.arange(768)
    order[(target % 384) // 24 * 48 + target // 384 * 24 + target % 24, target] = 1.0
    return jnp.asarray(order, BF16)


def shards(
    features,
    query_weight,
    key_weight,
    value_weight,
    output_weight,
    dilated_weight,
    mixing_weight,
    cotangent,
):
    core = lax.axis_index("dp") % 2
    flag = core.astype(jnp.int32).reshape(1)
    rows, slope = features.reshape(128, 768), cotangent.reshape(128, 768)
    (message,) = call(
        front,
        [(16, 360, 128)],
        flag,
        rows,
        dilated_weight,
        query_weight,
        key_weight,
        value_weight,
        fetched=((128, 768), (48, 1152), (768, 256), (768, 256), (768, 768)),
    )
    got = lax.all_to_all(message, "ctx", 0, 0)
    mixed, filters = call(attention, [(16, 120, 128), (384, 1152)], got, rows, slope, mixing_weight)
    others = other_core(filters)
    got = lax.all_to_all(mixed, "ctx", 0, 0)
    attended, gated, lifted, slopes, theirs = call(
        middle,
        [(128, 768), (128, 384), (128, 384), (128, 1152), (16, 216, 128)],
        flag,
        got,
        output_weight,
        filters,
        others,
        column_order(),
    )
    came = other_core(theirs)
    track, mine = call(
        rest, [(128, 768), (16, 216, 128)], attended, gated, mixing_weight, lifted, slopes
    )
    (message,) = call(joined, [(16, 264, 128)], mine, came, track)
    got = lax.all_to_all(message, "ctx", 0, 0)
    grad, track = call(summed, [(4, 112, 128), (128, 768)], got)
    got = lax.all_to_all(grad, "dp", 0, 0, axis_index_groups=NEAR)
    (grad,) = call(summed_again, [(4, 112, 128)], got)
    got = lax.all_to_all(grad, "dp", 0, 0, axis_index_groups=FAR)
    (grad,) = call(summed_again, [(4, 112, 128)], got)
    got = lax.all_to_all(grad, "dp", 0, 0, axis_index_groups=CLOSE)
    (dilated_grad,) = call(ordered, [(48, 1152)], got, dtype=F32)
    return (track.reshape(2, 64, 768), dilated_grad)


def solution(mesh):
    return jax.shard_map(
        shards,
        mesh=mesh,
        in_specs=(
            P("dp", "ctx", None),
            P(),
            P(),
            P(),
            P(),
            P("ctx", None),
            P(),
            P("dp", "ctx", None),
        ),
        out_specs=(P("dp", "ctx", None), P("ctx", None)),
        check_vma=False,
    )
```

```python
import math

import jax
import jax.numpy as jnp
from jax import lax
from jax.experimental import pallas as pl
from jax.experimental.pallas import tpu as pltpu
from jax.sharding import PartitionSpec as P


NEAR = [[2 * (4 * far + near) + core for near in range(4)] for core in range(2) for far in range(4)]
FAR = [[2 * (4 * far + near) + core for far in range(4)] for core in range(2) for near in range(4)]
CLOSE = [[4 * pair + member for member in range(4)] for pair in range(8)]
ACROSS = [[4 * y + x for x in range(4)] for y in range(4)]
F32, BF16 = jnp.float32, jnp.bfloat16
VMEM = pl.BlockSpec(memory_space=pltpu.VMEM)
SMEM = pl.BlockSpec(memory_space=pltpu.SMEM)


def dot(a, b, dims=((1,), (0,))):
    return lax.dot_general(a, b, (dims, ((), ())), preferred_element_type=F32)


def moves(count, source):
    row = lax.broadcasted_iota(jnp.int32, (count, count), 0)
    column = lax.broadcasted_iota(jnp.int32, (count, count), 1)
    return jnp.where(source(row, column), 1.0, 0.0).astype(BF16)


def layer_norm(values):
    center = values - jnp.mean(values, axis=-1, keepdims=True)
    spread = jnp.mean(center * center, axis=-1, keepdims=True)
    return center * lax.rsqrt(spread + 1e-05)


def head_norm(values):
    row = lax.broadcasted_iota(jnp.int32, (256, 256), 0)
    column = lax.broadcasted_iota(jnp.int32, (256, 256), 1)
    same = jnp.where((row >> 6) == (column >> 6), 1.0 / 64.0, 0.0).astype(BF16)
    square = values * values
    high = square.astype(BF16)
    mean = dot(high, same) + dot((square - high.astype(F32)).astype(BF16), same)
    return values * lax.rsqrt(mean + 1e-06)


def normal_cdf(values):
    return 0.5 * (1.0 + lax.erf(values * (1.0 / math.sqrt(2.0))))


def swap(tile):
    return pltpu.roll(tile, 64, 1)


def strips(rows, parts):
    lane = lax.broadcasted_iota(jnp.int32, (rows, 128), 1)
    result = jnp.zeros((rows, 128), F32)
    for tile, start, target, count in parts:
        if start != target:
            tile = pltpu.roll(tile, (target - start) % 128, 1)
        result = jnp.where((lane >= target) & (lane < target + count), tile, result)
    return result


def lower_lanes(rows):
    return lax.broadcasted_iota(jnp.int32, (rows, 128), 1) < 64


def fetch(pieces, semaphores):
    copies = [pltpu.make_async_copy(a, b, semaphores.at[n]) for n, (a, b) in enumerate(pieces)]
    for copy in copies:
        copy.start()
    return copies


def front(core, x, wd, wq, wk, wv, message, x_here, wd_here, wq_here, wk_here, wv_here, semaphores):
    pieces = [(x, x_here), (wd, wd_here)]
    for weight, here in ((wq, wq_here), (wk, wk_here), (wv, wv_here)):
        step = weight.shape[0] // 2
        pieces += [(weight.at[pl.ds(step * n, step)], here.at[pl.ds(step * n, step)]) for n in range(2)]
    copies = fetch(pieces, semaphores)
    to_queries = moves(128, lambda r, c: c == ((r >> 6) * 64 + ((r >> 1) & 15) * 4 + ((r >> 5) & 1) * 2 + (r & 1)))
    copies[0].wait()
    normed = layer_norm(x_here[...].astype(F32)).astype(BF16)
    copies[1].wait()
    tiles = [wd_here[:, 128 * k : 128 * k + 128].astype(F32) for k in range(9)]
    for x in range(4):
        block = [
            strips(48, [(tiles[4 * n + k], 32 * x, 32 * k, 32) for k in range(4)]) for n in range(2)
        ]
        block.append(strips(16, [(tiles[8][16 * m : 16 * m + 16], 32 * x, 32 * m, 32) for m in range(3)]))
        block = jnp.concatenate(block, axis=0).astype(BF16)
        for y in range(4):
            message[4 * y + x, 144:256, :] = block
    for copy in copies[2:4]:
        copy.wait()
    q = head_norm(dot(normed, wq_here[...]))
    q = dot(to_queries, q.astype(BF16))
    for copy in copies[4:6]:
        copy.wait()
    k = head_norm(dot(normed, wk_here[...]))
    for copy in copies[6:8]:
        copy.wait()
    v = dot(normed, wv_here[...])
    low16, low64 = lower_lanes(16), lower_lanes(64)
    for s in range(2):
        rows = slice(64 * s, 64 * s + 64)
        for pair in range(2):
            key = k[rows, 128 * pair : 128 * pair + 128]
            left, middle, right = (v[rows, 384 * pair + 128 * t : 384 * pair + 128 * t + 128] for t in range(3))
            for odd in range(2):
                first = jnp.where(low64, swap(key) if odd else key, middle if odd else swap(middle))
                block = jnp.concatenate([first, right if odd else left], axis=0).astype(BF16)
                for half in range(2):
                    message[8 * s + 4 * pair + 2 * odd + half, 0:128, :] = block
            for half in range(2):
                start = 64 * s + 32 * half
                a = q[start : start + 16, 128 * pair : 128 * pair + 128]
                b = q[start + 16 : start + 32, 128 * pair : 128 * pair + 128]
                message[8 * s + 4 * pair + half, 128:144, :] = jnp.where(low16, a, swap(b)).astype(BF16)
                message[8 * s + 4 * pair + 2 + half, 128:144, :] = jnp.where(low16, swap(a), b).astype(BF16)


def attention(got, x, cot, mix, out, filters):
    low = got[:, 0:64, :].reshape(1024, 128)
    high = got[:, 64:128, :].reshape(1024, 128)
    value = jnp.concatenate([low, high], axis=1)
    query = got[:, 128:144, :].reshape(256, 128)
    by_bins = moves(256, lambda r, c: c == (((r >> 1) & 15) * 16 + (r >> 5) * 2 + (r & 1)))
    query = dot(by_bins, query) * 0.25
    is_low = lower_lanes(256)
    queries = (jnp.where(is_low, query, 0.0).astype(BF16), jnp.where(is_low, swap(query), 0.0).astype(BF16))
    low16 = lower_lanes(16)
    for block in range(4):
        rows = queries[block // 2][128 * (block % 2) : 128 * (block % 2) + 128]
        weights = jnp.exp(dot(rows, low, ((1,), (1,))))
        total = jnp.sum(weights, axis=-1, keepdims=True)
        mixed = dot(weights.astype(BF16), value) / total
        for j in range(4):
            part = mixed[32 * j : 32 * j + 32]
            first = jnp.where(low16, swap(part[16:32, 0:128]), part[0:16, 0:128])
            out[4 * block + j, 0:48, :] = jnp.concatenate([first, part[:, 128:256]], axis=0).astype(BF16)
    first = got[:, 144:192, :].reshape(768, 128).astype(F32)
    second = got[:, 192:240, :].reshape(768, 128).astype(F32)
    last = got[:, 240:256, :].reshape(256, 128).astype(F32)
    thirds = [last, pltpu.roll(last, 96, 1), pltpu.roll(last, 64, 1)]
    last = jnp.concatenate([t[16 * i : 16 * i + 16] for i in range(16) for t in thirds], axis=0)
    filters[:, 0:128] = strips(768, [(first, 0, 0, 96)]).astype(BF16)
    filters[:, 128:256] = strips(768, [(first, 96, 0, 32), (second, 0, 32, 64)]).astype(BF16)
    filters[:, 256:384] = strips(768, [(second, 64, 0, 64), (last, 0, 64, 32)]).astype(BF16)
    to_bins = moves(128, lambda r, c: c == (((r >> 2) & 1) * 64 + (r >> 3) * 4 + (r & 3)))
    sent = dot(to_bins, x[...]).astype(BF16)
    for t in range(6):
        for j in range(16):
            out[j, 48 + 8 * t : 56 + 8 * t, :] = sent[8 * j : 8 * j + 8, 128 * t : 128 * t + 128]
    back = dot(dot(to_bins, cot[...]).astype(BF16), mix[...], ((1,), (1,)))
    for quarter in range(4):
        part = strips(128, [(back[:, 128 * t : 128 * t + 128], 32 * quarter, 32 * t, 32) for t in range(3)])
        part = part.astype(BF16)
        for y in range(4):
            out[4 * y + quarter, 96:128, :] = part[32 * y : 32 * y + 32]


def to_groups():
    return moves(128, lambda r, c: c == (((r >> 1) & 15) * 8 + (r >> 5) * 2 + (r & 1)))


def to_blocks():
    return moves(128, lambda r, c: c == (((r >> 1) & 3) * 32 + (r >> 3) * 2 + (r & 1)))


def attend(got, wo):
    sent = []
    for t in range(6):
        rows = [got[i, 48 + 8 * t : 56 + 8 * t, :].astype(F32) for i in range(16)]
        sent.append(jnp.concatenate(rows, axis=0).astype(BF16))
    sent = dot(to_groups(), jnp.concatenate(sent, axis=1))
    low16 = lower_lanes(16)
    tiles = []
    for pair in range(2):
        groups = [[], [], []]
        for s in range(2):
            for half in range(2):
                even, odd = (got[8 * s + 4 * pair + 2 * o + half, 0:48, :].astype(F32) for o in range(2))
                e, o = even[0:16], odd[0:16]
                groups[0].append(even[16:48])
                groups[1] += [jnp.where(low16, swap(e), o), jnp.where(low16, e, swap(o))]
                groups[2].append(odd[16:48])
        tiles += [jnp.concatenate(g, axis=0) for g in groups]
    mixed = jnp.concatenate(tiles, axis=1).astype(BF16)
    return (sent + dot(mixed, wo[...])).astype(BF16)


def middle(got, wo, lifted):
    normed = layer_norm(attend(got, wo).astype(F32))
    result = (normed * normal_cdf(normed)).astype(BF16)
    for x in range(4):
        lifted[x] = result


def filtered(core, lifted, got, filters, gated, mine, theirs):
    rows = lifted[...].reshape(512, 768)
    taps = dot(rows, filters[...])
    place = lax.broadcasted_iota(jnp.int32, (512, 128), 0) & 31

    def from_below(tile):
        return jnp.where(place >= 4, pltpu.roll(tile, 4, 0), 0.0)

    def from_above(tile):
        return jnp.where(place < 28, pltpu.roll(tile, 508, 0), 0.0)

    hidden = from_below(taps[:, 0:128]) + taps[:, 128:256] + from_above(taps[:, 256:384])
    cdf = normal_cdf(hidden)
    gated[...] = (hidden * cdf).astype(BF16)
    pdf = jnp.exp(-0.5 * hidden * hidden) * (1.0 / math.sqrt(2.0 * math.pi))
    back = []
    for x in range(4):
        part = [got[i, 96 + 8 * x : 104 + 8 * x, :].astype(F32) for i in range(16)]
        back.append(dot(to_groups(), jnp.concatenate(part, axis=0).astype(BF16)))
    slope = jnp.concatenate(back, axis=0) * (cdf + hidden * pdf)
    slope = slope.astype(BF16).astype(F32)
    below, above = from_above(slope), from_below(slope)
    packed = [
        strips(512, [(below, 0, 0, 96), (slope, 0, 96, 32)]),
        strips(512, [(slope, 32, 0, 64), (above, 0, 64, 64)]),
        strips(512, [(above, 64, 0, 32)]),
    ]
    packed = jnp.concatenate(packed, axis=1).astype(BF16)
    grad = dot(rows, packed, ((0,), (0,)))
    for d in range(16):
        halves = []
        for half in range(2):
            start = 48 * d + 24 * half
            part = grad[start : start + 24]
            last = strips(8, [(part[8 * m : 8 * m + 8, 256:384], 0, 32 * m, 32) for m in range(3)])
            halves.append(jnp.concatenate([part[:, 0:128], part[:, 128:256], last], axis=0))
        theirs[d] = jnp.where(core[0] == 0, halves[1], halves[0]).astype(BF16)
        mine[d] = jnp.where(core[0] == 0, halves[0], halves[1]).astype(BF16)


def rest(got, wo, gated, head):
    rows = dot(to_blocks(), attend(got, wo))
    gated = [dot(to_blocks(), gated[128 * x : 128 * x + 128, :]) for x in range(4)]
    gated = [strips(128, [(gated[m], 0, 0, 96), (gated[3], 32 * m, 96, 32)]) for m in range(3)]
    for i in range(16):
        block = slice(8 * i, 8 * i + 8)
        parts = [rows[block, 128 * t : 128 * t + 128] for t in range(6)] + [g[block] for g in gated]
        head[i] = jnp.concatenate(parts, axis=0).astype(BF16)


def joined(mine, came, head, message):
    for d in range(16):
        grad = mine[d].astype(F32) + came[d].astype(F32)
        message[d] = jnp.concatenate([grad, head[d].astype(F32)], axis=0).astype(BF16)


def summed(got, mix, grad, track):
    total = []
    for x in range(4):
        part = got[x, 0:56, :].astype(F32)
        for y in range(1, 4):
            part = part + got[4 * y + x, 0:56, :].astype(F32)
        total.append(part)
    for near in range(4):
        half = 2 * (near % 2)
        grad[near] = jnp.concatenate(total[half : half + 2], axis=0).astype(BF16)
    natural = moves(128, lambda r, c: c == (((r >> 2) & 15) * 8 + (r >> 6) * 4 + (r & 3)))
    gated, weights = [], []
    for x in range(4):
        rows = []
        for y in range(4):
            part = got[4 * y + x, 104:128, :].astype(F32)
            part = [part[8 * m : 8 * m + 8] for m in range(3)]
            rows += [strips(8, [(p, 0, 0, 96)]) for p in part]
            rows.append(strips(8, [(part[m], 96, 32 * m, 32) for m in range(3)]))
        gated.append(jnp.concatenate(rows, axis=0).astype(BF16))
        weights += [mix[128 * t + 32 * x : 128 * t + 32 * x + 32, :] for t in range(3)]
        weights.append(jnp.zeros((32, 768), BF16))
    attended = []
    for t in range(6):
        rows = [got[d, 56 + 8 * t : 64 + 8 * t, :].astype(F32) for d in range(16)]
        attended.append(jnp.concatenate(rows, axis=0).astype(BF16))
    gated = dot(natural, jnp.concatenate(gated, axis=1)).astype(BF16)
    attended = dot(natural, jnp.concatenate(attended, axis=1))
    track[...] = (attended + dot(gated, jnp.concatenate(weights, axis=0))).astype(BF16)


def summed_again(got, grad):
    total = got[0].astype(F32) + got[1].astype(F32) + got[2].astype(F32) + got[3].astype(F32)
    total = total.astype(BF16)
    for copy in range(grad.shape[0]):
        grad[copy] = total


def ordered(got, grad):
    for core in range(2):
        sources = []
        for x in range(4):
            part = got[2 * (x // 2) + core, 56 * (x % 2) : 56 * (x % 2) + 56, :].astype(F32)
            last = part[48:56]
            last = jnp.concatenate([last, pltpu.roll(last, 96, 1), pltpu.roll(last, 64, 1)], axis=0)
            sources.append((part[0:24], part[24:48], last))
        for k in range(9):
            tile = strips(24, [(sources[x][k // 4], 32 * (k % 4), 32 * x, 32) for x in range(4)])
            grad[24 * core : 24 * core + 24, 128 * k : 128 * k + 128] = tile


def call(kernel, outs, *args, dtype=BF16, fetched=()):
    scratch = [pltpu.VMEM(shape, BF16) for shape in fetched]
    if fetched:
        scratch.append(pltpu.SemaphoreType.DMA((8,)))
    return pl.pallas_call(
        kernel,
        out_shape=[jax.ShapeDtypeStruct(shape, dtype) for shape in outs],
        in_specs=[
            SMEM if a.dtype == jnp.int32 else pl.BlockSpec(memory_space=pl.ANY) if fetched else VMEM
            for a in args
        ],
        out_specs=[VMEM] * len(outs),
        scratch_shapes=scratch,
        compiler_params=pltpu.CompilerParams(vmem_limit_bytes=(56 if fetched else 32) * 1024 * 1024),
    )(*args)


def other_core(value):
    return lax.ppermute(value, "dp", [(source, source ^ 1) for source in range(32)])


def shards(
    features,
    query_weight,
    key_weight,
    value_weight,
    output_weight,
    dilated_weight,
    mixing_weight,
    cotangent,
):
    core = lax.axis_index("dp") % 2
    flag = core.astype(jnp.int32).reshape(1)
    rows, slope = features.reshape(128, 768), cotangent.reshape(128, 768)
    (message,) = call(
        front,
        [(16, 256, 128)],
        flag,
        rows,
        dilated_weight,
        query_weight,
        key_weight,
        value_weight,
        fetched=((128, 768), (48, 1152), (768, 256), (768, 256), (768, 768)),
    )
    got = lax.all_to_all(message, "ctx", 0, 0)
    mixed, filters = call(attention, [(16, 128, 128), (768, 384)], got, rows, slope, mixing_weight)
    got = lax.all_to_all(mixed, "ctx", 0, 0)
    (lifted,) = call(middle, [(4, 128, 768)], got, output_weight)
    lifted = lax.all_to_all(lifted, "ctx", 0, 0, axis_index_groups=ACROSS)
    gated, mine, theirs = call(
        filtered, [(512, 128), (16, 56, 128), (16, 56, 128)], flag, lifted, got, filters
    )
    came = other_core(theirs)
    (head,) = call(rest, [(16, 72, 128)], got, output_weight, gated)
    (message,) = call(joined, [(16, 128, 128)], mine, came, head)
    got = lax.all_to_all(message, "ctx", 0, 0)
    grad, track = call(summed, [(4, 112, 128), (128, 768)], got, mixing_weight)
    got = lax.all_to_all(grad, "dp", 0, 0, axis_index_groups=NEAR)
    (grad,) = call(summed_again, [(4, 112, 128)], got)
    got = lax.all_to_all(grad, "dp", 0, 0, axis_index_groups=FAR)
    (grad,) = call(summed_again, [(4, 112, 128)], got)
    got = lax.all_to_all(grad, "dp", 0, 0, axis_index_groups=CLOSE)
    (dilated_grad,) = call(ordered, [(48, 1152)], got, dtype=F32)
    return (track.reshape(2, 64, 768), dilated_grad)


def solution(mesh):
    return jax.shard_map(
        shards,
        mesh=mesh,
        in_specs=(
            P("dp", "ctx", None),
            P(),
            P(),
            P(),
            P(),
            P("ctx", None),
            P(),
            P("dp", "ctx", None),
        ),
        out_specs=(P("dp", "ctx", None), P("ctx", None)),
        check_vma=False,
    )
```

```python
import math

import jax
import jax.numpy as jnp
from jax import lax
from jax.experimental import pallas as pl
from jax.experimental.pallas import tpu as pltpu
from jax.sharding import PartitionSpec as P


NEAR = [[2 * (4 * far + near) + core for near in range(4)] for core in range(2) for far in range(4)]
FAR = [[2 * (4 * far + near) + core for far in range(4)] for core in range(2) for near in range(4)]
CLOSE = [[4 * pair + member for member in range(4)] for pair in range(8)]
ACROSS = [[4 * y + x for x in range(4)] for y in range(4)]
F32, BF16 = jnp.float32, jnp.bfloat16
VMEM = pl.BlockSpec(memory_space=pltpu.VMEM)
SMEM = pl.BlockSpec(memory_space=pltpu.SMEM)


def dot(a, b, dims=((1,), (0,))):
    return lax.dot_general(a, b, (dims, ((), ())), preferred_element_type=F32)


def moves(count, source):
    row = lax.broadcasted_iota(jnp.int32, (count, count), 0)
    column = lax.broadcasted_iota(jnp.int32, (count, count), 1)
    return jnp.where(source(row, column), 1.0, 0.0).astype(BF16)


def layer_norm(values):
    center = values - jnp.mean(values, axis=-1, keepdims=True)
    spread = jnp.mean(center * center, axis=-1, keepdims=True)
    return center * lax.rsqrt(spread + 1e-05)


def head_norm(values):
    row = lax.broadcasted_iota(jnp.int32, (256, 256), 0)
    column = lax.broadcasted_iota(jnp.int32, (256, 256), 1)
    same = jnp.where((row >> 6) == (column >> 6), 1.0 / 64.0, 0.0).astype(BF16)
    square = values * values
    high = square.astype(BF16)
    mean = dot(high, same) + dot((square - high.astype(F32)).astype(BF16), same)
    return values * lax.rsqrt(mean + 1e-06)


def normal_cdf(values):
    return 0.5 * (1.0 + lax.erf(values * (1.0 / math.sqrt(2.0))))


def swap(tile):
    return pltpu.roll(tile, 64, 1)


def strips(rows, parts):
    lane = lax.broadcasted_iota(jnp.int32, (rows, 128), 1)
    result = jnp.zeros((rows, 128), F32)
    for tile, start, target, count in parts:
        if start != target:
            tile = pltpu.roll(tile, (target - start) % 128, 1)
        result = jnp.where((lane >= target) & (lane < target + count), tile, result)
    return result


def lower_lanes(rows):
    return lax.broadcasted_iota(jnp.int32, (rows, 128), 1) < 64


def fetch(pieces, semaphores):
    copies = [pltpu.make_async_copy(a, b, semaphores.at[n]) for n, (a, b) in enumerate(pieces)]
    for copy in copies:
        copy.start()
    return copies


def front(core, x, wd, wq, wk, wv, message, x_here, wd_here, wq_here, wk_here, wv_here, semaphores):
    pieces = [(x, x_here), (wd, wd_here)]
    for weight, here in ((wq, wq_here), (wk, wk_here), (wv, wv_here)):
        step = weight.shape[0] // 2
        pieces += [(weight.at[pl.ds(step * n, step)], here.at[pl.ds(step * n, step)]) for n in range(2)]
    copies = fetch(pieces, semaphores)
    to_queries = moves(128, lambda r, c: c == ((r >> 6) * 64 + ((r >> 1) & 15) * 4 + ((r >> 5) & 1) * 2 + (r & 1)))
    copies[0].wait()
    normed = layer_norm(x_here[...].astype(F32)).astype(BF16)
    copies[1].wait()
    tiles = [wd_here[:, 128 * k : 128 * k + 128].astype(F32) for k in range(9)]
    for x in range(4):
        block = [
            strips(48, [(tiles[4 * n + k], 32 * x, 32 * k, 32) for k in range(4)]) for n in range(2)
        ]
        block.append(strips(16, [(tiles[8][16 * m : 16 * m + 16], 32 * x, 32 * m, 32) for m in range(3)]))
        block = jnp.concatenate(block, axis=0).astype(BF16)
        for y in range(4):
            message[4 * y + x, 144:256, :] = block
    for copy in copies[2:4]:
        copy.wait()
    q = head_norm(dot(normed, wq_here[...]))
    q = dot(to_queries, q.astype(BF16))
    for copy in copies[4:6]:
        copy.wait()
    k = head_norm(dot(normed, wk_here[...]))
    for copy in copies[6:8]:
        copy.wait()
    v = dot(normed, wv_here[...])
    low16, low64 = lower_lanes(16), lower_lanes(64)
    for s in range(2):
        rows = slice(64 * s, 64 * s + 64)
        for pair in range(2):
            key = k[rows, 128 * pair : 128 * pair + 128]
            left, middle, right = (v[rows, 384 * pair + 128 * t : 384 * pair + 128 * t + 128] for t in range(3))
            for odd in range(2):
                first = jnp.where(low64, swap(key) if odd else key, middle if odd else swap(middle))
                block = jnp.concatenate([first, right if odd else left], axis=0).astype(BF16)
                for half in range(2):
                    message[8 * s + 4 * pair + 2 * odd + half, 0:128, :] = block
            for half in range(2):
                start = 64 * s + 32 * half
                a = q[start : start + 16, 128 * pair : 128 * pair + 128]
                b = q[start + 16 : start + 32, 128 * pair : 128 * pair + 128]
                message[8 * s + 4 * pair + half, 128:144, :] = jnp.where(low16, a, swap(b)).astype(BF16)
                message[8 * s + 4 * pair + 2 + half, 128:144, :] = jnp.where(low16, swap(a), b).astype(BF16)


def attention(got, x, cot, mix, out, filters):
    low = got[:, 0:64, :].reshape(1024, 128)
    high = got[:, 64:128, :].reshape(1024, 128)
    value = jnp.concatenate([low, high], axis=1)
    query = got[:, 128:144, :].reshape(256, 128)
    by_bins = moves(256, lambda r, c: c == (((r >> 1) & 15) * 16 + (r >> 5) * 2 + (r & 1)))
    query = dot(by_bins, query) * 0.25
    is_low = lower_lanes(256)
    queries = (jnp.where(is_low, query, 0.0).astype(BF16), jnp.where(is_low, swap(query), 0.0).astype(BF16))
    low16 = lower_lanes(16)
    for block in range(4):
        rows = queries[block // 2][128 * (block % 2) : 128 * (block % 2) + 128]
        weights = jnp.exp(dot(rows, low, ((1,), (1,))))
        total = jnp.sum(weights, axis=-1, keepdims=True)
        mixed = dot(weights.astype(BF16), value) / total
        for j in range(4):
            part = mixed[32 * j : 32 * j + 32]
            first = jnp.where(low16, swap(part[16:32, 0:128]), part[0:16, 0:128])
            out[4 * block + j, 0:48, :] = jnp.concatenate([first, part[:, 128:256]], axis=0).astype(BF16)
    first = got[:, 144:192, :].reshape(768, 128).astype(F32)
    second = got[:, 192:240, :].reshape(768, 128).astype(F32)
    last = got[:, 240:256, :].reshape(256, 128).astype(F32)
    thirds = [last, pltpu.roll(last, 96, 1), pltpu.roll(last, 64, 1)]
    last = jnp.concatenate([t[16 * i : 16 * i + 16] for i in range(16) for t in thirds], axis=0)
    filters[:, 0:128] = strips(768, [(first, 0, 0, 96)]).astype(BF16)
    filters[:, 128:256] = strips(768, [(first, 96, 0, 32), (second, 0, 32, 64)]).astype(BF16)
    filters[:, 256:384] = strips(768, [(second, 64, 0, 64), (last, 0, 64, 32)]).astype(BF16)
    to_bins = moves(128, lambda r, c: c == (((r >> 2) & 1) * 64 + (r >> 3) * 4 + (r & 3)))
    sent = dot(to_bins, x[...]).astype(BF16)
    for t in range(6):
        for j in range(16):
            out[j, 48 + 8 * t : 56 + 8 * t, :] = sent[8 * j : 8 * j + 8, 128 * t : 128 * t + 128]
    back = dot(dot(to_bins, cot[...]).astype(BF16), mix[...], ((1,), (1,)))
    for quarter in range(4):
        part = strips(128, [(back[:, 128 * t : 128 * t + 128], 32 * quarter, 32 * t, 32) for t in range(3)])
        for y in range(4):
            rows = part[32 * y : 32 * y + 32]
            rows = [
                strips(8, [(rows[8 * m : 8 * m + 8], 0, 0, 96), (rows[24:32], 32 * m, 96, 32)]) for m in range(3)
            ]
            out[4 * y + quarter, 96:120, :] = jnp.concatenate(rows, axis=0).astype(BF16)


def to_groups():
    return moves(128, lambda r, c: c == (((r >> 1) & 15) * 8 + (r >> 5) * 2 + (r & 1)))


def to_blocks():
    return moves(128, lambda r, c: c == (((r >> 1) & 3) * 32 + (r >> 3) * 2 + (r & 1)))


def attend(got, wo):
    sent = []
    for t in range(6):
        rows = [got[i, 48 + 8 * t : 56 + 8 * t, :].astype(F32) for i in range(16)]
        sent.append(jnp.concatenate(rows, axis=0).astype(BF16))
    sent = dot(to_groups(), jnp.concatenate(sent, axis=1))
    low16 = lower_lanes(16)
    tiles = []
    for pair in range(2):
        groups = [[], [], []]
        for s in range(2):
            for half in range(2):
                even, odd = (got[8 * s + 4 * pair + 2 * o + half, 0:48, :].astype(F32) for o in range(2))
                e, o = even[0:16], odd[0:16]
                groups[0].append(even[16:48])
                groups[1] += [jnp.where(low16, swap(e), o), jnp.where(low16, e, swap(o))]
                groups[2].append(odd[16:48])
        tiles += [jnp.concatenate(g, axis=0) for g in groups]
    mixed = jnp.concatenate(tiles, axis=1).astype(BF16)
    return (sent + dot(mixed, wo[...])).astype(BF16)


def middle(got, wo, lifted):
    normed = layer_norm(attend(got, wo).astype(F32))
    result = (normed * normal_cdf(normed)).astype(BF16)
    for x in range(4):
        lifted[x] = result


def filtered(core, lifted, got, filters, gated, mine, theirs):
    rows = lifted[...].reshape(512, 768)
    taps = dot(rows, filters[...])
    place = lax.broadcasted_iota(jnp.int32, (512, 128), 0) & 31

    def from_below(tile):
        return jnp.where(place >= 4, pltpu.roll(tile, 4, 0), 0.0)

    def from_above(tile):
        return jnp.where(place < 28, pltpu.roll(tile, 508, 0), 0.0)

    hidden = from_below(taps[:, 0:128]) + taps[:, 128:256] + from_above(taps[:, 256:384])
    cdf = normal_cdf(hidden)
    gated[...] = (hidden * cdf).astype(BF16)
    pdf = jnp.exp(-0.5 * hidden * hidden) * (1.0 / math.sqrt(2.0 * math.pi))
    back = []
    came = [jnp.concatenate([got[i, 96 + 8 * m : 104 + 8 * m, :].astype(F32) for i in range(16)], axis=0) for m in range(3)]
    for x in range(4):
        part = [(came[x], 0, 0, 96)] if x < 3 else [(came[m], 96, 32 * m, 32) for m in range(3)]
        back.append(dot(to_groups(), strips(128, part).astype(BF16)))
    slope = jnp.concatenate(back, axis=0) * (cdf + hidden * pdf)
    slope = slope.astype(BF16).astype(F32)
    below, above = from_above(slope), from_below(slope)
    packed = [
        strips(512, [(below, 0, 0, 96), (slope, 0, 96, 32)]),
        strips(512, [(slope, 32, 0, 64), (above, 0, 64, 64)]),
        strips(512, [(above, 64, 0, 32)]),
    ]
    packed = jnp.concatenate(packed, axis=1).astype(BF16)
    grad = dot(rows, packed, ((0,), (0,)))
    for d in range(16):
        halves = []
        for half in range(2):
            start = 48 * d + 24 * half
            part = grad[start : start + 24]
            last = strips(8, [(part[8 * m : 8 * m + 8, 256:384], 0, 32 * m, 32) for m in range(3)])
            halves.append(jnp.concatenate([part[:, 0:128], part[:, 128:256], last], axis=0))
        theirs[d] = jnp.where(core[0] == 0, halves[1], halves[0]).astype(BF16)
        mine[d] = jnp.where(core[0] == 0, halves[0], halves[1]).astype(BF16)


def rest(got, wo, gated, message):
    rows = dot(to_blocks(), attend(got, wo))
    gated = [dot(to_blocks(), gated[128 * x : 128 * x + 128, :]) for x in range(4)]
    gated = [strips(128, [(gated[m], 0, 0, 96), (gated[3], 32 * m, 96, 32)]) for m in range(3)]
    for i in range(16):
        block = slice(8 * i, 8 * i + 8)
        parts = [rows[block, 128 * t : 128 * t + 128] for t in range(6)] + [g[block] for g in gated]
        message[i, 56:128, :] = jnp.concatenate(parts, axis=0).astype(BF16)


def joined(mine, came, begun, message):
    for d in range(16):
        message[d, 0:56, :] = (mine[d].astype(F32) + came[d].astype(F32)).astype(BF16)


def summed(got, mix, grad, track):
    total = []
    for x in range(4):
        part = got[x, 0:56, :].astype(F32)
        for y in range(1, 4):
            part = part + got[4 * y + x, 0:56, :].astype(F32)
        total.append(part)
    for near in range(4):
        half = 2 * (near % 2)
        grad[near] = jnp.concatenate(total[half : half + 2], axis=0).astype(BF16)
    natural = moves(128, lambda r, c: c == (((r >> 2) & 15) * 8 + (r >> 6) * 4 + (r & 3)))
    gated, weights = [], []
    for x in range(4):
        rows = []
        for y in range(4):
            part = got[4 * y + x, 104:128, :].astype(F32)
            part = [part[8 * m : 8 * m + 8] for m in range(3)]
            rows += [strips(8, [(p, 0, 0, 96)]) for p in part]
            rows.append(strips(8, [(part[m], 96, 32 * m, 32) for m in range(3)]))
        gated.append(jnp.concatenate(rows, axis=0).astype(BF16))
        weights += [mix[128 * t + 32 * x : 128 * t + 32 * x + 32, :] for t in range(3)]
        weights.append(jnp.zeros((32, 768), BF16))
    attended = []
    for t in range(6):
        rows = [got[d, 56 + 8 * t : 64 + 8 * t, :].astype(F32) for d in range(16)]
        attended.append(jnp.concatenate(rows, axis=0).astype(BF16))
    gated = dot(natural, jnp.concatenate(gated, axis=1)).astype(BF16)
    attended = dot(natural, jnp.concatenate(attended, axis=1))
    track[...] = (attended + dot(gated, jnp.concatenate(weights, axis=0))).astype(BF16)


def summed_again(got, grad):
    total = got[0].astype(F32) + got[1].astype(F32) + got[2].astype(F32) + got[3].astype(F32)
    total = total.astype(BF16)
    for copy in range(grad.shape[0]):
        grad[copy] = total


def ordered(got, rows, target, track, grad, semaphores):
    copies = [
        pltpu.make_async_copy(rows, track, semaphores.at[0]),
        pltpu.make_async_copy(grad, target, semaphores.at[1]),
    ]
    copies[0].start()
    for core in range(2):
        sources = []
        for x in range(4):
            part = got[2 * (x // 2) + core, 56 * (x % 2) : 56 * (x % 2) + 56, :].astype(F32)
            last = part[48:56]
            last = jnp.concatenate([last, pltpu.roll(last, 96, 1), pltpu.roll(last, 64, 1)], axis=0)
            sources.append((part[0:24], part[24:48], last))
        for k in range(9):
            tile = strips(24, [(sources[x][k // 4], 32 * (k % 4), 32 * x, 32) for x in range(4)])
            grad[24 * core : 24 * core + 24, 128 * k : 128 * k + 128] = tile
    copies[1].start()
    for copy in copies:
        copy.wait()


def call(kernel, outs, *args, fetched=(), copies=0, in_hbm=(), out_hbm=(), limit=32, alias={}):
    hbm = pl.BlockSpec(memory_space=pl.ANY)
    return pl.pallas_call(
        kernel,
        out_shape=[jax.ShapeDtypeStruct(out[1:], F32) if out[0] == F32 else jax.ShapeDtypeStruct(out, BF16) for out in outs],
        in_specs=[
            SMEM if a.dtype == jnp.int32 else hbm if n in in_hbm else VMEM for n, a in enumerate(args)
        ],
        out_specs=[hbm if n in out_hbm else VMEM for n in range(len(outs))],
        scratch_shapes=[
            pltpu.VMEM(shape[1:], F32) if shape[0] == F32 else pltpu.VMEM(shape, BF16) for shape in fetched
        ]
        + ([pltpu.SemaphoreType.DMA((copies,))] if copies else []),
        input_output_aliases=alias,
        compiler_params=pltpu.CompilerParams(vmem_limit_bytes=limit * 1024 * 1024),
    )(*args)


def other_core(value):
    return lax.ppermute(value, "dp", [(source, source ^ 1) for source in range(32)])


def shards(
    features,
    query_weight,
    key_weight,
    value_weight,
    output_weight,
    dilated_weight,
    mixing_weight,
    cotangent,
):
    core = lax.axis_index("dp") % 2
    flag = core.astype(jnp.int32).reshape(1)
    rows, slope = features.reshape(128, 768), cotangent.reshape(128, 768)
    (message,) = call(
        front,
        [(16, 256, 128)],
        flag,
        rows,
        dilated_weight,
        query_weight,
        key_weight,
        value_weight,
        fetched=((128, 768), (48, 1152), (768, 256), (768, 256), (768, 768)),
        copies=8,
        in_hbm=(1, 2, 3, 4, 5),
        limit=56,
    )
    got = lax.all_to_all(message, "ctx", 0, 0)
    mixed, filters = call(attention, [(16, 120, 128), (768, 384)], got, rows, slope, mixing_weight)
    got = lax.all_to_all(mixed, "ctx", 0, 0)
    (lifted,) = call(middle, [(4, 128, 768)], got, output_weight)
    lifted = lax.all_to_all(lifted, "ctx", 0, 0, axis_index_groups=ACROSS)
    gated, mine, theirs = call(
        filtered, [(512, 128), (16, 56, 128), (16, 56, 128)], flag, lifted, got, filters
    )
    came = other_core(theirs)
    (message,) = call(rest, [(16, 128, 128)], got, output_weight, gated)
    (message,) = call(joined, [(16, 128, 128)], mine, came, message, alias={2: 0})
    got = lax.all_to_all(message, "ctx", 0, 0)
    grad, track = call(summed, [(4, 112, 128), (128, 768)], got, mixing_weight)
    got = lax.all_to_all(grad, "dp", 0, 0, axis_index_groups=NEAR)
    (grad,) = call(summed_again, [(4, 112, 128)], got)
    got = lax.all_to_all(grad, "dp", 0, 0, axis_index_groups=FAR)
    (grad,) = call(summed_again, [(4, 112, 128)], got)
    got = lax.all_to_all(grad, "dp", 0, 0, axis_index_groups=CLOSE)
    dilated_grad, track = call(
        ordered, [(F32, 48, 1152), (128, 768)], got, track, fetched=((F32, 48, 1152),), copies=2, out_hbm=(0, 1)
    )
    return (track.reshape(2, 64, 768), dilated_grad)


def solution(mesh):
    return jax.shard_map(
        shards,
        mesh=mesh,
        in_specs=(
            P("dp", "ctx", None),
            P(),
            P(),
            P(),
            P(),
            P("ctx", None),
            P(),
            P("dp", "ctx", None),
        ),
        out_specs=(P("dp", "ctx", None), P("ctx", None)),
        check_vma=False,
    )
```

```python
import math

import jax
import jax.numpy as jnp
from jax import lax
from jax.experimental import pallas as pl
from jax.experimental.pallas import tpu as pltpu
from jax.sharding import PartitionSpec as P


NEAR = [[2 * (4 * far + near) + core for near in range(4)] for core in range(2) for far in range(4)]
FAR = [[2 * (4 * far + near) + core for far in range(4)] for core in range(2) for near in range(4)]
CLOSE = [[4 * pair + member for member in range(4)] for pair in range(8)]
CTX = [[16 * d + (k if d % 2 == 0 else 4 * (k % 4) + k // 4) for k in range(16)] for d in range(32)]
ACROSS = [[member for member in group[4 * a : 4 * a + 4]] for group in CTX for a in range(4)]
F32, BF16 = jnp.float32, jnp.bfloat16
VMEM = pl.BlockSpec(memory_space=pltpu.VMEM)
SMEM = pl.BlockSpec(memory_space=pltpu.SMEM)


def dot(a, b, dims=((1,), (0,))):
    return lax.dot_general(a, b, (dims, ((), ())), preferred_element_type=F32)


def moves(count, source):
    row = lax.broadcasted_iota(jnp.int32, (count, count), 0)
    column = lax.broadcasted_iota(jnp.int32, (count, count), 1)
    return jnp.where(source(row, column), 1.0, 0.0).astype(BF16)


def layer_norm(values):
    center = values - jnp.mean(values, axis=-1, keepdims=True)
    spread = jnp.mean(center * center, axis=-1, keepdims=True)
    return center * lax.rsqrt(spread + 1e-05)


def head_norm(values):
    row = lax.broadcasted_iota(jnp.int32, (256, 256), 0)
    column = lax.broadcasted_iota(jnp.int32, (256, 256), 1)
    same = jnp.where((row >> 6) == (column >> 6), 1.0 / 64.0, 0.0).astype(BF16)
    square = values * values
    high = square.astype(BF16)
    mean = dot(high, same) + dot((square - high.astype(F32)).astype(BF16), same)
    return values * lax.rsqrt(mean + 1e-06)


def normal_cdf(values):
    return 0.5 * (1.0 + lax.erf(values * (1.0 / math.sqrt(2.0))))


def swap(tile):
    return pltpu.roll(tile, 64, 1)


def strips(rows, parts):
    lane = lax.broadcasted_iota(jnp.int32, (rows, 128), 1)
    result = jnp.zeros((rows, 128), F32)
    for tile, start, target, count in parts:
        if start != target:
            tile = pltpu.roll(tile, (target - start) % 128, 1)
        result = jnp.where((lane >= target) & (lane < target + count), tile, result)
    return result


def slot(core, i):
    turned = 4 * (i % 4) + i // 4
    return i if turned == i else jnp.where(core[0] == 0, i, turned)


def lower_lanes(rows):
    return lax.broadcasted_iota(jnp.int32, (rows, 128), 1) < 64


def fetch(pieces, semaphores):
    copies = [pltpu.make_async_copy(a, b, semaphores.at[n]) for n, (a, b) in enumerate(pieces)]
    for copy in copies:
        copy.start()
    return copies


def front(core, x, wd, wq, wk, wv, message, x_here, wd_here, wq_here, wk_here, wv_here, semaphores):
    pieces = [(x, x_here), (wd, wd_here)]
    for weight, here in ((wq, wq_here), (wk, wk_here), (wv, wv_here)):
        step = weight.shape[0] // 2
        pieces += [(weight.at[pl.ds(step * n, step)], here.at[pl.ds(step * n, step)]) for n in range(2)]
    copies = fetch(pieces, semaphores)
    to_queries = moves(128, lambda r, c: c == ((r >> 6) * 64 + ((r >> 1) & 15) * 4 + ((r >> 5) & 1) * 2 + (r & 1)))
    copies[0].wait()
    normed = layer_norm(x_here[...].astype(F32)).astype(BF16)
    copies[1].wait()
    tiles = [wd_here[:, 128 * k : 128 * k + 128].astype(F32) for k in range(9)]
    for x in range(4):
        block = [
            strips(48, [(tiles[4 * n + k], 32 * x, 32 * k, 32) for k in range(4)]) for n in range(2)
        ]
        block.append(strips(16, [(tiles[8][16 * m : 16 * m + 16], 32 * x, 32 * m, 32) for m in range(3)]))
        block = jnp.concatenate(block, axis=0).astype(BF16)
        for y in range(4):
            message[4 * y + (x - y) % 4, 144:256, :] = block
    for copy in copies[2:4]:
        copy.wait()
    q = head_norm(dot(normed, wq_here[...]))
    q = dot(to_queries, q.astype(BF16))
    for copy in copies[4:6]:
        copy.wait()
    k = head_norm(dot(normed, wk_here[...]))
    for copy in copies[6:8]:
        copy.wait()
    v = dot(normed, wv_here[...])
    low16, low64 = lower_lanes(16), lower_lanes(64)
    for s in range(2):
        rows = slice(64 * s, 64 * s + 64)
        for pair in range(2):
            key = k[rows, 128 * pair : 128 * pair + 128]
            left, middle, right = (v[rows, 384 * pair + 128 * t : 384 * pair + 128 * t + 128] for t in range(3))
            for odd in range(2):
                first = jnp.where(low64, swap(key) if odd else key, middle if odd else swap(middle))
                block = jnp.concatenate([first, right if odd else left], axis=0).astype(BF16)
                for half in range(2):
                    message[8 * s + 4 * pair + 2 * odd + half, 0:128, :] = block
            for half in range(2):
                start = 64 * s + 32 * half
                a = q[start : start + 16, 128 * pair : 128 * pair + 128]
                b = q[start + 16 : start + 32, 128 * pair : 128 * pair + 128]
                message[8 * s + 4 * pair + half, 128:144, :] = jnp.where(low16, a, swap(b)).astype(BF16)
                message[8 * s + 4 * pair + 2 + half, 128:144, :] = jnp.where(low16, swap(a), b).astype(BF16)


def attention(core, got, x, cot, mix, out, filters):
    low = got[:, 0:64, :].reshape(1024, 128)
    high = got[:, 64:128, :].reshape(1024, 128)
    value = jnp.concatenate([low, high], axis=1)
    slots = [slot(core, i) for i in range(16)]
    query = jnp.concatenate([got[i, 128:144, :] for i in slots], axis=0)
    by_bins = moves(256, lambda r, c: c == (((r >> 1) & 15) * 16 + (r >> 5) * 2 + (r & 1)))
    query = dot(by_bins, query) * 0.25
    is_low = lower_lanes(256)
    queries = (jnp.where(is_low, query, 0.0).astype(BF16), jnp.where(is_low, swap(query), 0.0).astype(BF16))
    low16 = lower_lanes(16)
    for block in range(4):
        rows = queries[block // 2][128 * (block % 2) : 128 * (block % 2) + 128]
        weights = jnp.exp(dot(rows, low, ((1,), (1,))))
        total = jnp.sum(weights, axis=-1, keepdims=True)
        mixed = dot(weights.astype(BF16), value) / total
        for j in range(4):
            part = mixed[32 * j : 32 * j + 32]
            first = jnp.where(low16, swap(part[16:32, 0:128]), part[0:16, 0:128])
            out[4 * block + j, 0:48, :] = jnp.concatenate([first, part[:, 128:256]], axis=0).astype(BF16)
    first, second, last = (
        jnp.concatenate([got[i, start:stop, :].astype(F32) for i in slots], axis=0)
        for start, stop in ((144, 192), (192, 240), (240, 256))
    )
    thirds = [last, pltpu.roll(last, 96, 1), pltpu.roll(last, 64, 1)]
    last = jnp.concatenate([t[16 * i : 16 * i + 16] for i in range(16) for t in thirds], axis=0)
    filters[:, 0:128] = strips(768, [(first, 0, 0, 96)]).astype(BF16)
    filters[:, 128:256] = strips(768, [(first, 96, 0, 32), (second, 0, 32, 64)]).astype(BF16)
    filters[:, 256:384] = strips(768, [(second, 64, 0, 64), (last, 0, 64, 32)]).astype(BF16)
    to_bins = moves(128, lambda r, c: c == (((r >> 2) & 1) * 64 + (r >> 3) * 4 + (r & 3)))
    sent = dot(to_bins, x[...]).astype(BF16)
    for t in range(6):
        for j in range(16):
            out[j, 48 + 8 * t : 56 + 8 * t, :] = sent[8 * j : 8 * j + 8, 128 * t : 128 * t + 128]
    back = dot(dot(to_bins, cot[...]).astype(BF16), mix[...], ((1,), (1,)))
    for quarter in range(4):
        part = strips(128, [(back[:, 128 * t : 128 * t + 128], 32 * quarter, 32 * t, 32) for t in range(3)])
        for y in range(4):
            rows = part[32 * y : 32 * y + 32]
            rows = [
                strips(8, [(rows[8 * m : 8 * m + 8], 0, 0, 96), (rows[24:32], 32 * m, 96, 32)]) for m in range(3)
            ]
            out[4 * y + (quarter - y) % 4, 96:120, :] = jnp.concatenate(rows, axis=0).astype(BF16)


def to_groups():
    return moves(128, lambda r, c: c == (((r >> 1) & 15) * 8 + (r >> 5) * 2 + (r & 1)))


def to_blocks():
    return moves(128, lambda r, c: c == (((r >> 1) & 3) * 32 + (r >> 3) * 2 + (r & 1)))


def attend(core, got, wo):
    sent = []
    for t in range(6):
        rows = [got[slot(core, i), 48 + 8 * t : 56 + 8 * t, :].astype(F32) for i in range(16)]
        sent.append(jnp.concatenate(rows, axis=0).astype(BF16))
    sent = dot(to_groups(), jnp.concatenate(sent, axis=1))
    low16 = lower_lanes(16)
    tiles = []
    for pair in range(2):
        groups = [[], [], []]
        for s in range(2):
            for half in range(2):
                even, odd = (got[8 * s + 4 * pair + 2 * o + half, 0:48, :].astype(F32) for o in range(2))
                e, o = even[0:16], odd[0:16]
                groups[0].append(even[16:48])
                groups[1] += [jnp.where(low16, swap(e), o), jnp.where(low16, e, swap(o))]
                groups[2].append(odd[16:48])
        tiles += [jnp.concatenate(g, axis=0) for g in groups]
    mixed = jnp.concatenate(tiles, axis=1).astype(BF16)
    return (sent + dot(mixed, wo[...])).astype(BF16)


def middle(core, got, wo, lifted):
    normed = layer_norm(attend(core, got, wo).astype(F32))
    result = (normed * normal_cdf(normed)).astype(BF16)
    for x in range(4):
        lifted[x] = result


def filtered(core, lifted, got, filters, gated, mine, theirs):
    rows = lifted[...].reshape(512, 768)
    taps = dot(rows, filters[...])
    place = lax.broadcasted_iota(jnp.int32, (512, 128), 0) & 31

    def from_below(tile):
        return jnp.where(place >= 4, pltpu.roll(tile, 4, 0), 0.0)

    def from_above(tile):
        return jnp.where(place < 28, pltpu.roll(tile, 508, 0), 0.0)

    hidden = from_below(taps[:, 0:128]) + taps[:, 128:256] + from_above(taps[:, 256:384])
    cdf = normal_cdf(hidden)
    gated[...] = (hidden * cdf).astype(BF16)
    pdf = jnp.exp(-0.5 * hidden * hidden) * (1.0 / math.sqrt(2.0 * math.pi))
    back = []
    came = [jnp.concatenate([got[slot(core, i), 96 + 8 * m : 104 + 8 * m, :].astype(F32) for i in range(16)], axis=0) for m in range(3)]
    for x in range(4):
        part = [(came[x], 0, 0, 96)] if x < 3 else [(came[m], 96, 32 * m, 32) for m in range(3)]
        back.append(dot(to_groups(), strips(128, part).astype(BF16)))
    slope = jnp.concatenate(back, axis=0) * (cdf + hidden * pdf)
    slope = slope.astype(BF16).astype(F32)
    below, above = from_above(slope), from_below(slope)
    packed = [
        strips(512, [(below, 0, 0, 96), (slope, 0, 96, 32)]),
        strips(512, [(slope, 32, 0, 64), (above, 0, 64, 64)]),
        strips(512, [(above, 64, 0, 32)]),
    ]
    packed = jnp.concatenate(packed, axis=1).astype(BF16)
    grad = dot(rows, packed, ((0,), (0,)))
    for d in range(16):
        halves = []
        for half in range(2):
            start = 48 * d + 24 * half
            part = grad[start : start + 24]
            last = strips(8, [(part[8 * m : 8 * m + 8, 256:384], 0, 32 * m, 32) for m in range(3)])
            halves.append(jnp.concatenate([part[:, 0:128], part[:, 128:256], last], axis=0))
        theirs[d] = jnp.where(core[0] == 0, halves[1], halves[0]).astype(BF16)
        mine[d] = jnp.where(core[0] == 0, halves[0], halves[1]).astype(BF16)


def rest(core, got, wo, gated, message):
    rows = dot(to_blocks(), attend(core, got, wo))
    gated = [dot(to_blocks(), gated[128 * x : 128 * x + 128, :]) for x in range(4)]
    gated = [strips(128, [(gated[m], 0, 0, 96), (gated[3], 32 * m, 96, 32)]) for m in range(3)]
    for i in range(16):
        block = slice(8 * i, 8 * i + 8)
        parts = [rows[block, 128 * t : 128 * t + 128] for t in range(6)] + [g[block] for g in gated]
        message[slot(core, i), 56:128, :] = jnp.concatenate(parts, axis=0).astype(BF16)


def joined(core, mine, came, begun, message):
    for d in range(16):
        message[slot(core, d), 0:56, :] = (mine[d].astype(F32) + came[d].astype(F32)).astype(BF16)


def summed(got, mix, grad, track):
    total = []
    for x in range(4):
        part = got[x, 0:56, :].astype(F32)
        for y in range(1, 4):
            part = part + got[4 * y + (x - y) % 4, 0:56, :].astype(F32)
        total.append(part)
    for near in range(4):
        half = 2 * (near % 2)
        grad[near] = jnp.concatenate(total[half : half + 2], axis=0).astype(BF16)
    natural = moves(128, lambda r, c: c == (((r >> 2) & 15) * 8 + (r >> 6) * 4 + (r & 3)))
    gated, weights = [], []
    for x in range(4):
        rows = []
        for y in range(4):
            part = got[4 * y + (x - y) % 4, 104:128, :].astype(F32)
            part = [part[8 * m : 8 * m + 8] for m in range(3)]
            rows += [strips(8, [(p, 0, 0, 96)]) for p in part]
            rows.append(strips(8, [(part[m], 96, 32 * m, 32) for m in range(3)]))
        gated.append(jnp.concatenate(rows, axis=0).astype(BF16))
        weights += [mix[128 * t + 32 * x : 128 * t + 32 * x + 32, :] for t in range(3)]
        weights.append(jnp.zeros((32, 768), BF16))
    attended = []
    for t in range(6):
        rows = [got[d, 56 + 8 * t : 64 + 8 * t, :].astype(F32) for d in range(16)]
        attended.append(jnp.concatenate(rows, axis=0).astype(BF16))
    gated = dot(natural, jnp.concatenate(gated, axis=1)).astype(BF16)
    attended = dot(natural, jnp.concatenate(attended, axis=1))
    track[...] = (attended + dot(gated, jnp.concatenate(weights, axis=0))).astype(BF16)


def summed_again(got, grad):
    total = got[0].astype(F32) + got[1].astype(F32) + got[2].astype(F32) + got[3].astype(F32)
    total = total.astype(BF16)
    for copy in range(grad.shape[0]):
        grad[copy] = total


def ordered(got, rows, target, track, grad, semaphores):
    copies = [
        pltpu.make_async_copy(rows, track, semaphores.at[0]),
        pltpu.make_async_copy(grad, target, semaphores.at[1]),
    ]
    copies[0].start()
    for core in range(2):
        sources = []
        for x in range(4):
            part = got[2 * (x // 2) + core, 56 * (x % 2) : 56 * (x % 2) + 56, :].astype(F32)
            last = part[48:56]
            last = jnp.concatenate([last, pltpu.roll(last, 96, 1), pltpu.roll(last, 64, 1)], axis=0)
            sources.append((part[0:24], part[24:48], last))
        for k in range(9):
            tile = strips(24, [(sources[x][k // 4], 32 * (k % 4), 32 * x, 32) for x in range(4)])
            grad[24 * core : 24 * core + 24, 128 * k : 128 * k + 128] = tile
    copies[1].start()
    for copy in copies:
        copy.wait()


def call(kernel, outs, *args, fetched=(), copies=0, in_hbm=(), out_hbm=(), limit=32, alias={}):
    hbm = pl.BlockSpec(memory_space=pl.ANY)
    return pl.pallas_call(
        kernel,
        out_shape=[jax.ShapeDtypeStruct(out[1:], F32) if out[0] == F32 else jax.ShapeDtypeStruct(out, BF16) for out in outs],
        in_specs=[
            SMEM if a.dtype == jnp.int32 else hbm if n in in_hbm else VMEM for n, a in enumerate(args)
        ],
        out_specs=[hbm if n in out_hbm else VMEM for n in range(len(outs))],
        scratch_shapes=[
            pltpu.VMEM(shape[1:], F32) if shape[0] == F32 else pltpu.VMEM(shape, BF16) for shape in fetched
        ]
        + ([pltpu.SemaphoreType.DMA((copies,))] if copies else []),
        input_output_aliases=alias,
        compiler_params=pltpu.CompilerParams(vmem_limit_bytes=limit * 1024 * 1024),
    )(*args)


def other_core(value):
    return lax.ppermute(value, "dp", [(source, source ^ 1) for source in range(32)])


def shards(
    features,
    query_weight,
    key_weight,
    value_weight,
    output_weight,
    dilated_weight,
    mixing_weight,
    cotangent,
):
    core = lax.axis_index("dp") % 2
    flag = core.astype(jnp.int32).reshape(1)
    rows, slope = features.reshape(128, 768), cotangent.reshape(128, 768)
    (message,) = call(
        front,
        [(16, 256, 128)],
        flag,
        rows,
        dilated_weight,
        query_weight,
        key_weight,
        value_weight,
        fetched=((128, 768), (48, 1152), (768, 256), (768, 256), (768, 768)),
        copies=8,
        in_hbm=(1, 2, 3, 4, 5),
        limit=56,
    )
    got = lax.all_to_all(message, ("dp", "ctx"), 0, 0, axis_index_groups=CTX)
    mixed, filters = call(attention, [(16, 120, 128), (768, 384)], flag, got, rows, slope, mixing_weight)
    got = lax.all_to_all(mixed, ("dp", "ctx"), 0, 0, axis_index_groups=CTX)
    (lifted,) = call(middle, [(4, 128, 768)], flag, got, output_weight)
    lifted = lax.all_to_all(lifted, ("dp", "ctx"), 0, 0, axis_index_groups=ACROSS)
    gated, mine, theirs = call(
        filtered, [(512, 128), (16, 56, 128), (16, 56, 128)], flag, lifted, got, filters
    )
    came = other_core(theirs)
    (message,) = call(rest, [(16, 128, 128)], flag, got, output_weight, gated)
    (message,) = call(joined, [(16, 128, 128)], flag, mine, came, message, alias={3: 0})
    got = lax.all_to_all(message, ("dp", "ctx"), 0, 0, axis_index_groups=CTX)
    grad, track = call(summed, [(4, 112, 128), (128, 768)], got, mixing_weight)
    got = lax.all_to_all(grad, "dp", 0, 0, axis_index_groups=NEAR)
    (grad,) = call(summed_again, [(4, 112, 128)], got)
    got = lax.all_to_all(grad, "dp", 0, 0, axis_index_groups=FAR)
    (grad,) = call(summed_again, [(4, 112, 128)], got)
    got = lax.all_to_all(grad, "dp", 0, 0, axis_index_groups=CLOSE)
    dilated_grad, track = call(
        ordered, [(F32, 48, 1152), (128, 768)], got, track, fetched=((F32, 48, 1152),), copies=2, out_hbm=(0, 1)
    )
    return (track.reshape(2, 64, 768), dilated_grad)


def solution(mesh):
    return jax.shard_map(
        shards,
        mesh=mesh,
        in_specs=(
            P("dp", "ctx", None),
            P(),
            P(),
            P(),
            P(),
            P("ctx", None),
            P(),
            P("dp", "ctx", None),
        ),
        out_specs=(P("dp", "ctx", None), P("ctx", None)),
        check_vma=False,
    )
```

```python
import math

import jax
import jax.numpy as jnp
from jax import lax
from jax.experimental import pallas as pl
from jax.experimental.pallas import tpu as pltpu
from jax.sharding import PartitionSpec as P


NEAR = [[2 * (4 * far + near) + core for near in range(4)] for core in range(2) for far in range(4)]
FAR = [[2 * (4 * far + near) + core for far in range(4)] for core in range(2) for near in range(4)]
CLOSE = [[4 * pair + member for member in range(4)] for pair in range(8)]
CTX = [[16 * d + (k if d % 2 == 0 else 4 * (k % 4) + k // 4) for k in range(16)] for d in range(32)]
ACROSS = [[member for member in group[4 * a : 4 * a + 4]] for group in CTX for a in range(4)]
F32, BF16 = jnp.float32, jnp.bfloat16
VMEM = pl.BlockSpec(memory_space=pltpu.VMEM)
SMEM = pl.BlockSpec(memory_space=pltpu.SMEM)


def dot(a, b, dims=((1,), (0,))):
    return lax.dot_general(a, b, (dims, ((), ())), preferred_element_type=F32)


def moves(count, source):
    row = lax.broadcasted_iota(jnp.int32, (count, count), 0)
    column = lax.broadcasted_iota(jnp.int32, (count, count), 1)
    return jnp.where(source(row, column), 1.0, 0.0).astype(BF16)


def layer_norm(values):
    center = values - jnp.mean(values, axis=-1, keepdims=True)
    spread = jnp.mean(center * center, axis=-1, keepdims=True)
    return center * lax.rsqrt(spread + 1e-05)


def head_norm(values):
    row = lax.broadcasted_iota(jnp.int32, (256, 256), 0)
    column = lax.broadcasted_iota(jnp.int32, (256, 256), 1)
    same = jnp.where((row >> 6) == (column >> 6), 1.0 / 64.0, 0.0).astype(BF16)
    square = values * values
    high = square.astype(BF16)
    mean = dot(high, same) + dot((square - high.astype(F32)).astype(BF16), same)
    return values * lax.rsqrt(mean + 1e-06)


def normal_cdf(values):
    return 0.5 * (1.0 + lax.erf(values * (1.0 / math.sqrt(2.0))))


def swap(tile):
    return pltpu.roll(tile, 64, 1)


def strips(rows, parts):
    lane = lax.broadcasted_iota(jnp.int32, (rows, 128), 1)
    result = jnp.zeros((rows, 128), F32)
    for tile, start, target, count in parts:
        if start != target:
            tile = pltpu.roll(tile, (target - start) % 128, 1)
        result = jnp.where((lane >= target) & (lane < target + count), tile, result)
    return result


def slot(core, i):
    turned = 4 * (i % 4) + i // 4
    return i if turned == i else jnp.where(core[0] == 0, i, turned)


def lower_lanes(rows):
    return lax.broadcasted_iota(jnp.int32, (rows, 128), 1) < 64


def fetch(pieces, semaphores):
    copies = [pltpu.make_async_copy(a, b, semaphores.at[n]) for n, (a, b) in enumerate(pieces)]
    for copy in copies:
        copy.start()
    return copies


def front(core, x, wd, wq, wk, wv, message, x_here, wd_here, wq_here, wk_here, wv_here, semaphores):
    pieces = [(x, x_here), (wd, wd_here)]
    for weight, here in ((wq, wq_here), (wk, wk_here), (wv, wv_here)):
        step = weight.shape[0] // 2
        pieces += [(weight.at[pl.ds(step * n, step)], here.at[pl.ds(step * n, step)]) for n in range(2)]
    copies = fetch(pieces, semaphores)
    to_queries = moves(128, lambda r, c: c == ((r >> 6) * 64 + ((r >> 1) & 15) * 4 + ((r >> 5) & 1) * 2 + (r & 1)))
    copies[0].wait()
    normed = layer_norm(x_here[...].astype(F32)).astype(BF16)
    copies[1].wait()
    tiles = [wd_here[:, 128 * k : 128 * k + 128].astype(F32) for k in range(9)]
    for x in range(4):
        block = [
            strips(48, [(tiles[4 * n + k], 32 * x, 32 * k, 32) for k in range(4)]) for n in range(2)
        ]
        block.append(strips(16, [(tiles[8][16 * m : 16 * m + 16], 32 * x, 32 * m, 32) for m in range(3)]))
        block = jnp.concatenate(block, axis=0).astype(BF16)
        for y in range(4):
            message[4 * y + (x - y) % 4, 144:256, :] = block
    for copy in copies[2:4]:
        copy.wait()
    q = head_norm(dot(normed, wq_here[...]))
    q = dot(to_queries, q.astype(BF16))
    for copy in copies[4:6]:
        copy.wait()
    k = head_norm(dot(normed, wk_here[...]))
    for copy in copies[6:8]:
        copy.wait()
    v = dot(normed, wv_here[...])
    low16, low64 = lower_lanes(16), lower_lanes(64)
    for s in range(2):
        rows = slice(64 * s, 64 * s + 64)
        for pair in range(2):
            key = k[rows, 128 * pair : 128 * pair + 128]
            left, middle, right = (v[rows, 384 * pair + 128 * t : 384 * pair + 128 * t + 128] for t in range(3))
            for odd in range(2):
                first = jnp.where(low64, swap(key) if odd else key, middle if odd else swap(middle))
                block = jnp.concatenate([first, right if odd else left], axis=0).astype(BF16)
                for half in range(2):
                    message[8 * s + 4 * pair + 2 * odd + half, 0:128, :] = block
            for half in range(2):
                start = 64 * s + 32 * half
                a = q[start : start + 16, 128 * pair : 128 * pair + 128]
                b = q[start + 16 : start + 32, 128 * pair : 128 * pair + 128]
                message[8 * s + 4 * pair + half, 128:144, :] = jnp.where(low16, a, swap(b)).astype(BF16)
                message[8 * s + 4 * pair + 2 + half, 128:144, :] = jnp.where(low16, swap(a), b).astype(BF16)


def attention(core, got, x, cot, mix, out, filters):
    low = got[:, 0:64, :].reshape(1024, 128)
    high = got[:, 64:128, :].reshape(1024, 128)
    value = jnp.concatenate([low, high], axis=1)
    slots = [slot(core, i) for i in range(16)]
    query = jnp.concatenate([got[i, 128:144, :] for i in slots], axis=0)
    by_bins = moves(256, lambda r, c: c == (((r >> 1) & 15) * 16 + (r >> 5) * 2 + (r & 1)))
    query = dot(by_bins, query) * 0.25
    is_low = lower_lanes(256)
    queries = (jnp.where(is_low, query, 0.0).astype(BF16), jnp.where(is_low, swap(query), 0.0).astype(BF16))
    low16 = lower_lanes(16)
    for block in range(4):
        rows = queries[block // 2][128 * (block % 2) : 128 * (block % 2) + 128]
        weights = jnp.exp(dot(rows, low, ((1,), (1,))))
        total = jnp.sum(weights, axis=-1, keepdims=True)
        mixed = dot(weights.astype(BF16), value) / total
        for j in range(4):
            part = mixed[32 * j : 32 * j + 32]
            first = jnp.where(low16, swap(part[16:32, 0:128]), part[0:16, 0:128])
            out[4 * block + j, 0:48, :] = jnp.concatenate([first, part[:, 128:256]], axis=0).astype(BF16)
    first, second, last = (
        jnp.concatenate([got[i, start:stop, :].astype(F32) for i in slots], axis=0)
        for start, stop in ((144, 192), (192, 240), (240, 256))
    )
    thirds = [last, pltpu.roll(last, 96, 1), pltpu.roll(last, 64, 1)]
    last = jnp.concatenate([t[16 * i : 16 * i + 16] for i in range(16) for t in thirds], axis=0)
    filters[:, 0:128] = strips(768, [(first, 0, 0, 96)]).astype(BF16)
    filters[:, 128:256] = strips(768, [(first, 96, 0, 32), (second, 0, 32, 64)]).astype(BF16)
    filters[:, 256:384] = strips(768, [(second, 64, 0, 64), (last, 0, 64, 32)]).astype(BF16)
    to_bins = moves(128, lambda r, c: c == (((r >> 2) & 1) * 64 + (r >> 3) * 4 + (r & 3)))
    sent = dot(to_bins, x[...]).astype(BF16)
    for t in range(6):
        for j in range(16):
            out[j, 48 + 8 * t : 56 + 8 * t, :] = sent[8 * j : 8 * j + 8, 128 * t : 128 * t + 128]
    back = dot(dot(to_bins, cot[...]).astype(BF16), mix[...], ((1,), (1,)))
    for quarter in range(4):
        part = strips(128, [(back[:, 128 * t : 128 * t + 128], 32 * quarter, 32 * t, 32) for t in range(3)])
        for y in range(4):
            rows = part[32 * y : 32 * y + 32]
            rows = [
                strips(8, [(rows[8 * m : 8 * m + 8], 0, 0, 96), (rows[24:32], 32 * m, 96, 32)]) for m in range(3)
            ]
            out[4 * y + (quarter - y) % 4, 96:120, :] = jnp.concatenate(rows, axis=0).astype(BF16)


def to_groups():
    return moves(128, lambda r, c: c == (((r >> 1) & 15) * 8 + (r >> 5) * 2 + (r & 1)))


def to_blocks():
    return moves(128, lambda r, c: c == (((r >> 1) & 3) * 32 + (r >> 3) * 2 + (r & 1)))


def attend(core, got, wo):
    sent = []
    for t in range(6):
        rows = [got[slot(core, i), 48 + 8 * t : 56 + 8 * t, :].astype(F32) for i in range(16)]
        sent.append(jnp.concatenate(rows, axis=0).astype(BF16))
    sent = dot(to_groups(), jnp.concatenate(sent, axis=1))
    low16 = lower_lanes(16)
    tiles = []
    for pair in range(2):
        groups = [[], [], []]
        for s in range(2):
            for half in range(2):
                even, odd = (got[8 * s + 4 * pair + 2 * o + half, 0:48, :].astype(F32) for o in range(2))
                e, o = even[0:16], odd[0:16]
                groups[0].append(even[16:48])
                groups[1] += [jnp.where(low16, swap(e), o), jnp.where(low16, e, swap(o))]
                groups[2].append(odd[16:48])
        tiles += [jnp.concatenate(g, axis=0) for g in groups]
    mixed = jnp.concatenate(tiles, axis=1).astype(BF16)
    return (sent + dot(mixed, wo[...])).astype(BF16)


def middle(core, got, wo, lifted):
    normed = layer_norm(attend(core, got, wo).astype(F32))
    result = (normed * normal_cdf(normed)).astype(BF16)
    for x in range(4):
        lifted[x] = result


def filtered(core, lifted, got, filters, gated, slopes, theirs):
    rows = lifted[...].reshape(512, 768)
    taps = dot(rows, filters[...])
    place = lax.broadcasted_iota(jnp.int32, (512, 128), 0) & 31

    def from_below(tile):
        return jnp.where(place >= 4, pltpu.roll(tile, 4, 0), 0.0)

    def from_above(tile):
        return jnp.where(place < 28, pltpu.roll(tile, 508, 0), 0.0)

    hidden = from_below(taps[:, 0:128]) + taps[:, 128:256] + from_above(taps[:, 256:384])
    cdf = normal_cdf(hidden)
    gated[...] = (hidden * cdf).astype(BF16)
    pdf = jnp.exp(-0.5 * hidden * hidden) * (1.0 / math.sqrt(2.0 * math.pi))
    back = []
    came = [jnp.concatenate([got[slot(core, i), 96 + 8 * m : 104 + 8 * m, :].astype(F32) for i in range(16)], axis=0) for m in range(3)]
    for x in range(4):
        part = [(came[x], 0, 0, 96)] if x < 3 else [(came[m], 96, 32 * m, 32) for m in range(3)]
        back.append(dot(to_groups(), strips(128, part).astype(BF16)))
    slope = jnp.concatenate(back, axis=0) * (cdf + hidden * pdf)
    slope = slope.astype(BF16).astype(F32)
    below, above = from_above(slope), from_below(slope)
    packed = [
        strips(512, [(below, 0, 0, 96), (slope, 0, 96, 32)]),
        strips(512, [(slope, 32, 0, 64), (above, 0, 64, 64)]),
        strips(512, [(above, 64, 0, 32)]),
    ]
    slopes[...] = jnp.concatenate(packed, axis=1).astype(BF16)
    gradient(core, 1, rows, slopes, theirs)


def gradient(core, other, rows, slopes, target):
    grad = dot(rows, slopes[...], ((0,), (0,)))
    for d in range(16):
        low, high = grad[48 * d : 48 * d + 24], grad[48 * d + 24 : 48 * d + 48]
        part = jnp.where(core[0] == other, low, high)
        last = strips(8, [(part[8 * m : 8 * m + 8, 256:384], 0, 32 * m, 32) for m in range(3)])
        target[d] = jnp.concatenate([part[:, 0:128], part[:, 128:256], last], axis=0).astype(BF16)


def rest(core, got, wo, gated, lifted, slopes, message, mine):
    rows = dot(to_blocks(), attend(core, got, wo))
    gated = [dot(to_blocks(), gated[128 * x : 128 * x + 128, :]) for x in range(4)]
    gated = [strips(128, [(gated[m], 0, 0, 96), (gated[3], 32 * m, 96, 32)]) for m in range(3)]
    for i in range(16):
        block = slice(8 * i, 8 * i + 8)
        parts = [rows[block, 128 * t : 128 * t + 128] for t in range(6)] + [g[block] for g in gated]
        message[slot(core, i), 56:128, :] = jnp.concatenate(parts, axis=0).astype(BF16)
    gradient(core, 0, lifted[...].reshape(512, 768), slopes, mine)


def joined(core, mine, came, begun, message):
    for d in range(16):
        message[slot(core, d), 0:56, :] = (mine[d].astype(F32) + came[d].astype(F32)).astype(BF16)


def summed(got, mix, grad, track):
    total = []
    for x in range(4):
        part = got[x, 0:56, :].astype(F32)
        for y in range(1, 4):
            part = part + got[4 * y + (x - y) % 4, 0:56, :].astype(F32)
        total.append(part)
    for near in range(4):
        half = 2 * (near % 2)
        grad[near] = jnp.concatenate(total[half : half + 2], axis=0).astype(BF16)
    natural = moves(128, lambda r, c: c == (((r >> 2) & 15) * 8 + (r >> 6) * 4 + (r & 3)))
    gated, weights = [], []
    for x in range(4):
        rows = []
        for y in range(4):
            part = got[4 * y + (x - y) % 4, 104:128, :].astype(F32)
            part = [part[8 * m : 8 * m + 8] for m in range(3)]
            rows += [strips(8, [(p, 0, 0, 96)]) for p in part]
            rows.append(strips(8, [(part[m], 96, 32 * m, 32) for m in range(3)]))
        gated.append(jnp.concatenate(rows, axis=0).astype(BF16))
        weights += [mix[128 * t + 32 * x : 128 * t + 32 * x + 32, :] for t in range(3)]
        weights.append(jnp.zeros((32, 768), BF16))
    attended = []
    for t in range(6):
        rows = [got[d, 56 + 8 * t : 64 + 8 * t, :].astype(F32) for d in range(16)]
        attended.append(jnp.concatenate(rows, axis=0).astype(BF16))
    gated = dot(natural, jnp.concatenate(gated, axis=1)).astype(BF16)
    attended = dot(natural, jnp.concatenate(attended, axis=1))
    track[...] = (attended + dot(gated, jnp.concatenate(weights, axis=0))).astype(BF16)


def summed_again(got, grad):
    total = got[0].astype(F32) + got[1].astype(F32) + got[2].astype(F32) + got[3].astype(F32)
    total = total.astype(BF16)
    for copy in range(grad.shape[0]):
        grad[copy] = total


def ordered(got, rows, target, track, grad, semaphores):
    copies = [
        pltpu.make_async_copy(rows, track, semaphores.at[0]),
        pltpu.make_async_copy(grad, target, semaphores.at[1]),
    ]
    copies[0].start()
    for core in range(2):
        sources = []
        for x in range(4):
            part = got[2 * (x // 2) + core, 56 * (x % 2) : 56 * (x % 2) + 56, :].astype(F32)
            last = part[48:56]
            last = jnp.concatenate([last, pltpu.roll(last, 96, 1), pltpu.roll(last, 64, 1)], axis=0)
            sources.append((part[0:24], part[24:48], last))
        for k in range(9):
            tile = strips(24, [(sources[x][k // 4], 32 * (k % 4), 32 * x, 32) for x in range(4)])
            grad[24 * core : 24 * core + 24, 128 * k : 128 * k + 128] = tile
    copies[1].start()
    for copy in copies:
        copy.wait()


def call(kernel, outs, *args, fetched=(), copies=0, in_hbm=(), out_hbm=(), limit=32, alias={}):
    hbm = pl.BlockSpec(memory_space=pl.ANY)
    return pl.pallas_call(
        kernel,
        out_shape=[jax.ShapeDtypeStruct(out[1:], F32) if out[0] == F32 else jax.ShapeDtypeStruct(out, BF16) for out in outs],
        in_specs=[
            SMEM if a.dtype == jnp.int32 else hbm if n in in_hbm else VMEM for n, a in enumerate(args)
        ],
        out_specs=[hbm if n in out_hbm else VMEM for n in range(len(outs))],
        scratch_shapes=[
            pltpu.VMEM(shape[1:], F32) if shape[0] == F32 else pltpu.VMEM(shape, BF16) for shape in fetched
        ]
        + ([pltpu.SemaphoreType.DMA((copies,))] if copies else []),
        input_output_aliases=alias,
        compiler_params=pltpu.CompilerParams(vmem_limit_bytes=limit * 1024 * 1024),
    )(*args)


def other_core(value):
    return lax.ppermute(value, "dp", [(source, source ^ 1) for source in range(32)])


def shards(
    features,
    query_weight,
    key_weight,
    value_weight,
    output_weight,
    dilated_weight,
    mixing_weight,
    cotangent,
):
    core = lax.axis_index("dp") % 2
    flag = core.astype(jnp.int32).reshape(1)
    rows, slope = features.reshape(128, 768), cotangent.reshape(128, 768)
    (message,) = call(
        front,
        [(16, 256, 128)],
        flag,
        rows,
        dilated_weight,
        query_weight,
        key_weight,
        value_weight,
        fetched=((128, 768), (48, 1152), (768, 256), (768, 256), (768, 768)),
        copies=8,
        in_hbm=(1, 2, 3, 4, 5),
        limit=56,
    )
    got = lax.all_to_all(message, ("dp", "ctx"), 0, 0, axis_index_groups=CTX)
    mixed, filters = call(attention, [(16, 120, 128), (768, 384)], flag, got, rows, slope, mixing_weight)
    got = lax.all_to_all(mixed, ("dp", "ctx"), 0, 0, axis_index_groups=CTX)
    (lifted,) = call(middle, [(4, 128, 768)], flag, got, output_weight)
    lifted = lax.all_to_all(lifted, ("dp", "ctx"), 0, 0, axis_index_groups=ACROSS)
    gated, slopes, theirs = call(
        filtered, [(512, 128), (512, 384), (16, 56, 128)], flag, lifted, got, filters
    )
    came = other_core(theirs)
    message, mine = call(
        rest, [(16, 128, 128), (16, 56, 128)], flag, got, output_weight, gated, lifted, slopes
    )
    (message,) = call(joined, [(16, 128, 128)], flag, mine, came, message, alias={3: 0})
    got = lax.all_to_all(message, ("dp", "ctx"), 0, 0, axis_index_groups=CTX)
    grad, track = call(summed, [(4, 112, 128), (128, 768)], got, mixing_weight)
    got = lax.all_to_all(grad, "dp", 0, 0, axis_index_groups=NEAR)
    (grad,) = call(summed_again, [(4, 112, 128)], got)
    got = lax.all_to_all(grad, "dp", 0, 0, axis_index_groups=FAR)
    (grad,) = call(summed_again, [(4, 112, 128)], got)
    got = lax.all_to_all(grad, "dp", 0, 0, axis_index_groups=CLOSE)
    dilated_grad, track = call(
        ordered, [(F32, 48, 1152), (128, 768)], got, track, fetched=((F32, 48, 1152),), copies=2, out_hbm=(0, 1)
    )
    return (track.reshape(2, 64, 768), dilated_grad)


def solution(mesh):
    return jax.shard_map(
        shards,
        mesh=mesh,
        in_specs=(
            P("dp", "ctx", None),
            P(),
            P(),
            P(),
            P(),
            P("ctx", None),
            P(),
            P("dp", "ctx", None),
        ),
        out_specs=(P("dp", "ctx", None), P("ctx", None)),
        check_vma=False,
    )
```

```python
import math

import jax
import jax.numpy as jnp
from jax import lax
from jax.experimental import pallas as pl
from jax.experimental.pallas import tpu as pltpu
from jax.sharding import PartitionSpec as P


NEAR = [[2 * (4 * far + near) + core for near in range(4)] for core in range(2) for far in range(4)]
FAR = [[2 * (4 * far + near) + core for far in range(4)] for core in range(2) for near in range(4)]
CLOSE = [[4 * pair + member for member in range(4)] for pair in range(8)]
CTX = [[16 * d + (k if d % 2 == 0 else 4 * (k % 4) + k // 4) for k in range(16)] for d in range(32)]
ACROSS = [[member for member in group[4 * a : 4 * a + 4]] for group in CTX for a in range(4)]
F32, BF16 = jnp.float32, jnp.bfloat16
VMEM = pl.BlockSpec(memory_space=pltpu.VMEM)
SMEM = pl.BlockSpec(memory_space=pltpu.SMEM)


def dot(a, b, dims=((1,), (0,))):
    return lax.dot_general(a, b, (dims, ((), ())), preferred_element_type=F32)


def moves(count, source):
    row = lax.broadcasted_iota(jnp.int32, (count, count), 0)
    column = lax.broadcasted_iota(jnp.int32, (count, count), 1)
    return jnp.where(source(row, column), 1.0, 0.0).astype(BF16)


def layer_norm(values):
    center = values - jnp.mean(values, axis=-1, keepdims=True)
    spread = jnp.mean(center * center, axis=-1, keepdims=True)
    return center * lax.rsqrt(spread + 1e-05)


def head_norm(values):
    row = lax.broadcasted_iota(jnp.int32, (256, 256), 0)
    column = lax.broadcasted_iota(jnp.int32, (256, 256), 1)
    same = jnp.where((row >> 6) == (column >> 6), 1.0 / 64.0, 0.0).astype(BF16)
    square = values * values
    high = square.astype(BF16)
    mean = dot(high, same) + dot((square - high.astype(F32)).astype(BF16), same)
    return values * lax.rsqrt(mean + 1e-06)


def normal_cdf(values):
    return 0.5 * (1.0 + lax.erf(values * (1.0 / math.sqrt(2.0))))


def swap(tile):
    return pltpu.roll(tile, 64, 1)


def strips(rows, parts):
    lane = lax.broadcasted_iota(jnp.int32, (rows, 128), 1)
    result = jnp.zeros((rows, 128), F32)
    for tile, start, target, count in parts:
        if start != target:
            tile = pltpu.roll(tile, (target - start) % 128, 1)
        result = jnp.where((lane >= target) & (lane < target + count), tile, result)
    return result


def slot(core, i):
    turned = 4 * (i % 4) + i // 4
    return i if turned == i else jnp.where(core[0] == 0, i, turned)


def lower_lanes(rows):
    return lax.broadcasted_iota(jnp.int32, (rows, 128), 1) < 64


def fetch(pieces, semaphores):
    copies = [pltpu.make_async_copy(a, b, semaphores.at[n]) for n, (a, b) in enumerate(pieces)]
    for copy in copies:
        copy.start()
    return copies


def front(core, x, wd, wq, wk, wv, message, x_here, wd_here, wq_here, wk_here, wv_here, semaphores):
    copies = fetch([(x, x_here), (wd, wd_here), (wq, wq_here), (wk, wk_here), (wv, wv_here)], semaphores)
    to_queries = moves(128, lambda r, c: c == ((r >> 6) * 64 + ((r >> 1) & 15) * 4 + ((r >> 5) & 1) * 2 + (r & 1)))
    copies[0].wait()
    normed = layer_norm(x_here[...].astype(F32)).astype(BF16)
    copies[1].wait()
    tiles = [wd_here[:, 128 * k : 128 * k + 128].astype(F32) for k in range(9)]
    for x in range(4):
        block = [
            strips(48, [(tiles[4 * n + k], 32 * x, 32 * k, 32) for k in range(4)]) for n in range(2)
        ]
        block.append(strips(16, [(tiles[8][16 * m : 16 * m + 16], 32 * x, 32 * m, 32) for m in range(3)]))
        block = jnp.concatenate(block, axis=0).astype(BF16)
        for y in range(4):
            message[4 * y + (x - y) % 4, 144:256, :] = block
    copies[2].wait()
    q = head_norm(dot(normed, wq_here[...]))
    q = dot(to_queries, q.astype(BF16))
    copies[3].wait()
    k = head_norm(dot(normed, wk_here[...]))
    copies[4].wait()
    v = dot(normed, wv_here[...])
    low16, low64 = lower_lanes(16), lower_lanes(64)
    for s in range(2):
        rows = slice(64 * s, 64 * s + 64)
        for pair in range(2):
            key = k[rows, 128 * pair : 128 * pair + 128]
            left, middle, right = (v[rows, 384 * pair + 128 * t : 384 * pair + 128 * t + 128] for t in range(3))
            for odd in range(2):
                first = jnp.where(low64, swap(key) if odd else key, middle if odd else swap(middle))
                block = jnp.concatenate([first, right if odd else left], axis=0).astype(BF16)
                for half in range(2):
                    message[8 * s + 4 * pair + 2 * odd + half, 0:128, :] = block
            for half in range(2):
                start = 64 * s + 32 * half
                a = q[start : start + 16, 128 * pair : 128 * pair + 128]
                b = q[start + 16 : start + 32, 128 * pair : 128 * pair + 128]
                message[8 * s + 4 * pair + half, 128:144, :] = jnp.where(low16, a, swap(b)).astype(BF16)
                message[8 * s + 4 * pair + 2 + half, 128:144, :] = jnp.where(low16, swap(a), b).astype(BF16)


def attention(core, got, x, cot, mix, out, filters):
    low = got[:, 0:64, :].reshape(1024, 128)
    high = got[:, 64:128, :].reshape(1024, 128)
    value = jnp.concatenate([low, high], axis=1)
    slots = [slot(core, i) for i in range(16)]
    query = jnp.concatenate([got[i, 128:144, :] for i in slots], axis=0)
    by_bins = moves(256, lambda r, c: c == (((r >> 1) & 15) * 16 + (r >> 5) * 2 + (r & 1)))
    query = dot(by_bins, query) * 0.25
    is_low = lower_lanes(256)
    queries = (jnp.where(is_low, query, 0.0).astype(BF16), jnp.where(is_low, swap(query), 0.0).astype(BF16))
    low16 = lower_lanes(16)
    for block in range(4):
        rows = queries[block // 2][128 * (block % 2) : 128 * (block % 2) + 128]
        weights = jnp.exp(dot(rows, low, ((1,), (1,))))
        total = jnp.sum(weights, axis=-1, keepdims=True)
        mixed = dot(weights.astype(BF16), value) / total
        for j in range(4):
            part = mixed[32 * j : 32 * j + 32]
            first = jnp.where(low16, swap(part[16:32, 0:128]), part[0:16, 0:128])
            out[4 * block + j, 0:48, :] = jnp.concatenate([first, part[:, 128:256]], axis=0).astype(BF16)
    first, second, last = (
        jnp.concatenate([got[i, start:stop, :].astype(F32) for i in slots], axis=0)
        for start, stop in ((144, 192), (192, 240), (240, 256))
    )
    thirds = [last, pltpu.roll(last, 96, 1), pltpu.roll(last, 64, 1)]
    last = jnp.concatenate([t[16 * i : 16 * i + 16] for i in range(16) for t in thirds], axis=0)
    filters[:, 0:128] = strips(768, [(first, 0, 0, 96)]).astype(BF16)
    filters[:, 128:256] = strips(768, [(first, 96, 0, 32), (second, 0, 32, 64)]).astype(BF16)
    filters[:, 256:384] = strips(768, [(second, 64, 0, 64), (last, 0, 64, 32)]).astype(BF16)
    to_bins = moves(128, lambda r, c: c == (((r >> 2) & 1) * 64 + (r >> 3) * 4 + (r & 3)))
    sent = dot(to_bins, x[...]).astype(BF16)
    for t in range(6):
        for j in range(16):
            out[j, 48 + 8 * t : 56 + 8 * t, :] = sent[8 * j : 8 * j + 8, 128 * t : 128 * t + 128]
    back = dot(dot(to_bins, cot[...]).astype(BF16), mix[...], ((1,), (1,)))
    for quarter in range(4):
        part = strips(128, [(back[:, 128 * t : 128 * t + 128], 32 * quarter, 32 * t, 32) for t in range(3)])
        for y in range(4):
            rows = part[32 * y : 32 * y + 32]
            rows = [
                strips(8, [(rows[8 * m : 8 * m + 8], 0, 0, 96), (rows[24:32], 32 * m, 96, 32)]) for m in range(3)
            ]
            out[4 * y + (quarter - y) % 4, 96:120, :] = jnp.concatenate(rows, axis=0).astype(BF16)


def to_groups():
    return moves(128, lambda r, c: c == (((r >> 1) & 15) * 8 + (r >> 5) * 2 + (r & 1)))


def to_blocks():
    return moves(128, lambda r, c: c == (((r >> 1) & 3) * 32 + (r >> 3) * 2 + (r & 1)))


def attend(core, got, wo):
    sent = []
    for t in range(6):
        rows = [got[slot(core, i), 48 + 8 * t : 56 + 8 * t, :].astype(F32) for i in range(16)]
        sent.append(jnp.concatenate(rows, axis=0).astype(BF16))
    sent = dot(to_groups(), jnp.concatenate(sent, axis=1))
    low16 = lower_lanes(16)
    tiles = []
    for pair in range(2):
        groups = [[], [], []]
        for s in range(2):
            for half in range(2):
                even, odd = (got[8 * s + 4 * pair + 2 * o + half, 0:48, :].astype(F32) for o in range(2))
                e, o = even[0:16], odd[0:16]
                groups[0].append(even[16:48])
                groups[1] += [jnp.where(low16, swap(e), o), jnp.where(low16, e, swap(o))]
                groups[2].append(odd[16:48])
        tiles += [jnp.concatenate(g, axis=0) for g in groups]
    mixed = jnp.concatenate(tiles, axis=1).astype(BF16)
    return (sent + dot(mixed, wo[...])).astype(BF16)


def middle(core, got, wo, lifted):
    normed = layer_norm(attend(core, got, wo).astype(F32))
    result = (normed * normal_cdf(normed)).astype(BF16)
    for x in range(4):
        lifted[x] = result


def filtered(core, lifted, got, filters, gated, mine, theirs):
    rows = lifted[...].reshape(512, 768)
    taps = dot(rows, filters[...])
    place = lax.broadcasted_iota(jnp.int32, (512, 128), 0) & 31

    def from_below(tile):
        return jnp.where(place >= 4, pltpu.roll(tile, 4, 0), 0.0)

    def from_above(tile):
        return jnp.where(place < 28, pltpu.roll(tile, 508, 0), 0.0)

    hidden = from_below(taps[:, 0:128]) + taps[:, 128:256] + from_above(taps[:, 256:384])
    cdf = normal_cdf(hidden)
    gated[...] = (hidden * cdf).astype(BF16)
    pdf = jnp.exp(-0.5 * hidden * hidden) * (1.0 / math.sqrt(2.0 * math.pi))
    back = []
    came = [jnp.concatenate([got[slot(core, i), 96 + 8 * m : 104 + 8 * m, :].astype(F32) for i in range(16)], axis=0) for m in range(3)]
    for x in range(4):
        part = [(came[x], 0, 0, 96)] if x < 3 else [(came[m], 96, 32 * m, 32) for m in range(3)]
        back.append(dot(to_groups(), strips(128, part).astype(BF16)))
    slope = jnp.concatenate(back, axis=0) * (cdf + hidden * pdf)
    slope = slope.astype(BF16).astype(F32)
    below, above = from_above(slope), from_below(slope)
    packed = [
        strips(512, [(below, 0, 0, 96), (slope, 0, 96, 32)]),
        strips(512, [(slope, 32, 0, 64), (above, 0, 64, 64)]),
        strips(512, [(above, 64, 0, 32)]),
    ]
    packed = jnp.concatenate(packed, axis=1).astype(BF16)
    grad = dot(rows, packed, ((0,), (0,)))
    for d in range(16):
        halves = []
        for half in range(2):
            start = 48 * d + 24 * half
            part = grad[start : start + 24]
            last = strips(8, [(part[8 * m : 8 * m + 8, 256:384], 0, 32 * m, 32) for m in range(3)])
            halves.append(jnp.concatenate([part[:, 0:128], part[:, 128:256], last], axis=0))
        theirs[d] = jnp.where(core[0] == 0, halves[1], halves[0]).astype(BF16)
        mine[d] = jnp.where(core[0] == 0, halves[0], halves[1]).astype(BF16)


def rest(core, got, wo, gated, message):
    rows = dot(to_blocks(), attend(core, got, wo))
    gated = [dot(to_blocks(), gated[128 * x : 128 * x + 128, :]) for x in range(4)]
    gated = [strips(128, [(gated[m], 0, 0, 96), (gated[3], 32 * m, 96, 32)]) for m in range(3)]
    for i in range(16):
        block = slice(8 * i, 8 * i + 8)
        parts = [rows[block, 128 * t : 128 * t + 128] for t in range(6)] + [g[block] for g in gated]
        message[slot(core, i), 56:128, :] = jnp.concatenate(parts, axis=0).astype(BF16)


def joined(core, mine, came, begun, message):
    for d in range(16):
        message[slot(core, d), 0:56, :] = (mine[d].astype(F32) + came[d].astype(F32)).astype(BF16)


def summed(got, mix, grad, track):
    total = []
    for x in range(4):
        part = got[x, 0:56, :].astype(F32)
        for y in range(1, 4):
            part = part + got[4 * y + (x - y) % 4, 0:56, :].astype(F32)
        total.append(part)
    for near in range(4):
        half = 2 * (near % 2)
        grad[near] = jnp.concatenate(total[half : half + 2], axis=0).astype(BF16)
    natural = moves(128, lambda r, c: c == (((r >> 2) & 15) * 8 + (r >> 6) * 4 + (r & 3)))
    gated, weights = [], []
    for x in range(4):
        rows = []
        for y in range(4):
            part = got[4 * y + (x - y) % 4, 104:128, :].astype(F32)
            part = [part[8 * m : 8 * m + 8] for m in range(3)]
            rows += [strips(8, [(p, 0, 0, 96)]) for p in part]
            rows.append(strips(8, [(part[m], 96, 32 * m, 32) for m in range(3)]))
        gated.append(jnp.concatenate(rows, axis=0).astype(BF16))
        weights += [mix[128 * t + 32 * x : 128 * t + 32 * x + 32, :] for t in range(3)]
        weights.append(jnp.zeros((32, 768), BF16))
    attended = []
    for t in range(6):
        rows = [got[d, 56 + 8 * t : 64 + 8 * t, :].astype(F32) for d in range(16)]
        attended.append(jnp.concatenate(rows, axis=0).astype(BF16))
    gated = dot(natural, jnp.concatenate(gated, axis=1)).astype(BF16)
    attended = dot(natural, jnp.concatenate(attended, axis=1))
    track[...] = (attended + dot(gated, jnp.concatenate(weights, axis=0))).astype(BF16)


def summed_again(got, grad):
    total = got[0].astype(F32) + got[1].astype(F32) + got[2].astype(F32) + got[3].astype(F32)
    total = total.astype(BF16)
    for copy in range(grad.shape[0]):
        grad[copy] = total


def ordered(got, rows, target, track, grad, semaphores):
    copies = [
        pltpu.make_async_copy(rows, track, semaphores.at[0]),
        pltpu.make_async_copy(grad, target, semaphores.at[1]),
    ]
    copies[0].start()
    for core in range(2):
        sources = []
        for x in range(4):
            part = got[2 * (x // 2) + core, 56 * (x % 2) : 56 * (x % 2) + 56, :].astype(F32)
            last = part[48:56]
            last = jnp.concatenate([last, pltpu.roll(last, 96, 1), pltpu.roll(last, 64, 1)], axis=0)
            sources.append((part[0:24], part[24:48], last))
        for k in range(9):
            tile = strips(24, [(sources[x][k // 4], 32 * (k % 4), 32 * x, 32) for x in range(4)])
            grad[24 * core : 24 * core + 24, 128 * k : 128 * k + 128] = tile
    copies[1].start()
    for copy in copies:
        copy.wait()


def call(kernel, outs, *args, fetched=(), copies=0, in_hbm=(), out_hbm=(), limit=32, alias={}):
    hbm = pl.BlockSpec(memory_space=pl.ANY)
    return pl.pallas_call(
        kernel,
        out_shape=[jax.ShapeDtypeStruct(out[1:], F32) if out[0] == F32 else jax.ShapeDtypeStruct(out, BF16) for out in outs],
        in_specs=[
            SMEM if a.dtype == jnp.int32 else hbm if n in in_hbm else VMEM for n, a in enumerate(args)
        ],
        out_specs=[hbm if n in out_hbm else VMEM for n in range(len(outs))],
        scratch_shapes=[
            pltpu.VMEM(shape[1:], F32) if shape[0] == F32 else pltpu.VMEM(shape, BF16) for shape in fetched
        ]
        + ([pltpu.SemaphoreType.DMA((copies,))] if copies else []),
        input_output_aliases=alias,
        compiler_params=pltpu.CompilerParams(vmem_limit_bytes=limit * 1024 * 1024),
    )(*args)


def other_core(value):
    return lax.ppermute(value, "dp", [(source, source ^ 1) for source in range(32)])


def shards(
    features,
    query_weight,
    key_weight,
    value_weight,
    output_weight,
    dilated_weight,
    mixing_weight,
    cotangent,
):
    core = lax.axis_index("dp") % 2
    flag = core.astype(jnp.int32).reshape(1)
    rows, slope = features.reshape(128, 768), cotangent.reshape(128, 768)
    (message,) = call(
        front,
        [(16, 256, 128)],
        flag,
        rows,
        dilated_weight,
        query_weight,
        key_weight,
        value_weight,
        fetched=((128, 768), (48, 1152), (768, 256), (768, 256), (768, 768)),
        copies=5,
        in_hbm=(1, 2, 3, 4, 5),
        limit=56,
    )
    got = lax.all_to_all(message, ("dp", "ctx"), 0, 0, axis_index_groups=CTX)
    mixed, filters = call(attention, [(16, 120, 128), (768, 384)], flag, got, rows, slope, mixing_weight)
    got = lax.all_to_all(mixed, ("dp", "ctx"), 0, 0, axis_index_groups=CTX)
    (lifted,) = call(middle, [(4, 128, 768)], flag, got, output_weight)
    lifted = lax.all_to_all(lifted, ("dp", "ctx"), 0, 0, axis_index_groups=ACROSS)
    gated, mine, theirs = call(
        filtered, [(512, 128), (16, 56, 128), (16, 56, 128)], flag, lifted, got, filters
    )
    came = other_core(theirs)
    (message,) = call(rest, [(16, 128, 128)], flag, got, output_weight, gated)
    (message,) = call(joined, [(16, 128, 128)], flag, mine, came, message, alias={3: 0})
    got = lax.all_to_all(message, ("dp", "ctx"), 0, 0, axis_index_groups=CTX)
    grad, track = call(summed, [(4, 112, 128), (128, 768)], got, mixing_weight)
    got = lax.all_to_all(grad, "dp", 0, 0, axis_index_groups=NEAR)
    (grad,) = call(summed_again, [(4, 112, 128)], got)
    got = lax.all_to_all(grad, "dp", 0, 0, axis_index_groups=FAR)
    (grad,) = call(summed_again, [(4, 112, 128)], got)
    got = lax.all_to_all(grad, "dp", 0, 0, axis_index_groups=CLOSE)
    dilated_grad, track = call(
        ordered, [(F32, 48, 1152), (128, 768)], got, track, fetched=((F32, 48, 1152),), copies=2, out_hbm=(0, 1)
    )
    return (track.reshape(2, 64, 768), dilated_grad)


def solution(mesh):
    return jax.shard_map(
        shards,
        mesh=mesh,
        in_specs=(
            P("dp", "ctx", None),
            P(),
            P(),
            P(),
            P(),
            P("ctx", None),
            P(),
            P("dp", "ctx", None),
        ),
        out_specs=(P("dp", "ctx", None), P("ctx", None)),
        check_vma=False,
    )
```

```python
import math

import jax
import jax.numpy as jnp
from jax import lax
from jax.experimental import pallas as pl
from jax.experimental.pallas import tpu as pltpu
from jax.sharding import PartitionSpec as P


NEAR = [[2 * (4 * far + near) + core for near in range(4)] for core in range(2) for far in range(4)]
FAR = [[2 * (4 * far + near) + core for far in range(4)] for core in range(2) for near in range(4)]
CLOSE = [[4 * pair + member for member in range(4)] for pair in range(8)]
CTX = [[16 * d + (k if d % 2 == 0 else 4 * (k % 4) + k // 4) for k in range(16)] for d in range(32)]
ACROSS = [[member for member in group[4 * a : 4 * a + 4]] for group in CTX for a in range(4)]
F32, BF16 = jnp.float32, jnp.bfloat16
VMEM = pl.BlockSpec(memory_space=pltpu.VMEM)
SMEM = pl.BlockSpec(memory_space=pltpu.SMEM)


def dot(a, b, dims=((1,), (0,))):
    return lax.dot_general(a, b, (dims, ((), ())), preferred_element_type=F32)


def moves(count, source):
    row = lax.broadcasted_iota(jnp.int32, (count, count), 0)
    column = lax.broadcasted_iota(jnp.int32, (count, count), 1)
    return jnp.where(source(row, column), 1.0, 0.0).astype(BF16)


def layer_norm(values):
    center = values - jnp.mean(values, axis=-1, keepdims=True)
    spread = jnp.mean(center * center, axis=-1, keepdims=True)
    return center * lax.rsqrt(spread + 1e-05)


def head_norm(values):
    row = lax.broadcasted_iota(jnp.int32, (256, 256), 0)
    column = lax.broadcasted_iota(jnp.int32, (256, 256), 1)
    same = jnp.where((row >> 6) == (column >> 6), 1.0 / 64.0, 0.0).astype(BF16)
    square = values * values
    high = square.astype(BF16)
    mean = dot(high, same) + dot((square - high.astype(F32)).astype(BF16), same)
    return values * lax.rsqrt(mean + 1e-06)


def normal_cdf(values):
    return 0.5 * (1.0 + lax.erf(values * (1.0 / math.sqrt(2.0))))


def swap(tile):
    return pltpu.roll(tile, 64, 1)


def strips(rows, parts):
    lane = lax.broadcasted_iota(jnp.int32, (rows, 128), 1)
    result = jnp.zeros((rows, 128), F32)
    for tile, start, target, count in parts:
        if start != target:
            tile = pltpu.roll(tile, (target - start) % 128, 1)
        result = jnp.where((lane >= target) & (lane < target + count), tile, result)
    return result


def slot(core, i):
    turned = 4 * (i % 4) + i // 4
    return i if turned == i else jnp.where(core[0] == 0, i, turned)


def lower_lanes(rows):
    return lax.broadcasted_iota(jnp.int32, (rows, 128), 1) < 64


def fetch(pieces, semaphores):
    copies = [pltpu.make_async_copy(a, b, semaphores.at[n]) for n, (a, b) in enumerate(pieces)]
    for copy in copies:
        copy.start()
    return copies


def front(core, x, wd, wq, wk, wv, message, x_here, wd_here, wq_here, wk_here, wv_here, semaphores):
    pieces = [(x, x_here), (wd, wd_here)]
    for weight, here in ((wq, wq_here), (wk, wk_here), (wv, wv_here)):
        step = weight.shape[0] // 2
        pieces += [(weight.at[pl.ds(step * n, step)], here.at[pl.ds(step * n, step)]) for n in range(2)]
    copies = fetch(pieces, semaphores)
    to_queries = moves(128, lambda r, c: c == ((r >> 6) * 64 + ((r >> 1) & 15) * 4 + ((r >> 5) & 1) * 2 + (r & 1)))
    copies[0].wait()
    normed = layer_norm(x_here[...].astype(F32)).astype(BF16)
    copies[1].wait()
    tiles = [wd_here[:, 128 * k : 128 * k + 128].astype(F32) for k in range(9)]
    for x in range(4):
        block = [
            strips(48, [(tiles[4 * n + k], 32 * x, 32 * k, 32) for k in range(4)]) for n in range(2)
        ]
        block.append(strips(16, [(tiles[8][16 * m : 16 * m + 16], 32 * x, 32 * m, 32) for m in range(3)]))
        block = jnp.concatenate(block, axis=0).astype(BF16)
        for y in range(4):
            message[4 * y + (x - y) % 4, 144:256, :] = block
    for copy in copies[2:4]:
        copy.wait()
    for copy in copies[4:6]:
        copy.wait()
    both = jnp.concatenate([dot(normed, wq_here[...]), dot(normed, wk_here[...])], axis=0)
    both = head_norm(both)
    q, k = dot(to_queries, both[0:128].astype(BF16)), both[128:256]
    for copy in copies[6:8]:
        copy.wait()
    v = dot(normed, wv_here[...])
    low16, low64 = lower_lanes(16), lower_lanes(64)
    for s in range(2):
        rows = slice(64 * s, 64 * s + 64)
        for pair in range(2):
            key = k[rows, 128 * pair : 128 * pair + 128]
            left, middle, right = (v[rows, 384 * pair + 128 * t : 384 * pair + 128 * t + 128] for t in range(3))
            for odd in range(2):
                first = jnp.where(low64, swap(key) if odd else key, middle if odd else swap(middle))
                block = jnp.concatenate([first, right if odd else left], axis=0).astype(BF16)
                for half in range(2):
                    message[8 * s + 4 * pair + 2 * odd + half, 0:128, :] = block
            for half in range(2):
                start = 64 * s + 32 * half
                a = q[start : start + 16, 128 * pair : 128 * pair + 128]
                b = q[start + 16 : start + 32, 128 * pair : 128 * pair + 128]
                message[8 * s + 4 * pair + half, 128:144, :] = jnp.where(low16, a, swap(b)).astype(BF16)
                message[8 * s + 4 * pair + 2 + half, 128:144, :] = jnp.where(low16, swap(a), b).astype(BF16)


def attention(core, got, x, cot, mix, out, filters):
    low = got[:, 0:64, :].reshape(1024, 128)
    high = got[:, 64:128, :].reshape(1024, 128)
    value = jnp.concatenate([low, high], axis=1)
    slots = [slot(core, i) for i in range(16)]
    query = jnp.concatenate([got[i, 128:144, :] for i in slots], axis=0)
    by_bins = moves(256, lambda r, c: c == (((r >> 1) & 15) * 16 + (r >> 5) * 2 + (r & 1)))
    query = dot(by_bins, query) * 0.25
    is_low = lower_lanes(256)
    queries = (jnp.where(is_low, query, 0.0).astype(BF16), jnp.where(is_low, swap(query), 0.0).astype(BF16))
    low16 = lower_lanes(16)
    for block in range(4):
        rows = queries[block // 2][128 * (block % 2) : 128 * (block % 2) + 128]
        weights = jnp.exp(dot(rows, low, ((1,), (1,))))
        total = jnp.sum(weights, axis=-1, keepdims=True)
        mixed = dot(weights.astype(BF16), value) / total
        for j in range(4):
            part = mixed[32 * j : 32 * j + 32]
            first = jnp.where(low16, swap(part[16:32, 0:128]), part[0:16, 0:128])
            out[4 * block + j, 0:48, :] = jnp.concatenate([first, part[:, 128:256]], axis=0).astype(BF16)
    first, second, last = (
        jnp.concatenate([got[i, start:stop, :].astype(F32) for i in slots], axis=0)
        for start, stop in ((144, 192), (192, 240), (240, 256))
    )
    thirds = [last, pltpu.roll(last, 96, 1), pltpu.roll(last, 64, 1)]
    last = jnp.concatenate([t[16 * i : 16 * i + 16] for i in range(16) for t in thirds], axis=0)
    filters[:, 0:128] = strips(768, [(first, 0, 0, 96)]).astype(BF16)
    filters[:, 128:256] = strips(768, [(first, 96, 0, 32), (second, 0, 32, 64)]).astype(BF16)
    filters[:, 256:384] = strips(768, [(second, 64, 0, 64), (last, 0, 64, 32)]).astype(BF16)
    to_bins = moves(128, lambda r, c: c == (((r >> 2) & 1) * 64 + (r >> 3) * 4 + (r & 3)))
    sent = dot(to_bins, x[...]).astype(BF16)
    for t in range(6):
        for j in range(16):
            out[j, 48 + 8 * t : 56 + 8 * t, :] = sent[8 * j : 8 * j + 8, 128 * t : 128 * t + 128]
    back = dot(dot(to_bins, cot[...]).astype(BF16), mix[...], ((1,), (1,)))
    for quarter in range(4):
        part = strips(128, [(back[:, 128 * t : 128 * t + 128], 32 * quarter, 32 * t, 32) for t in range(3)])
        for y in range(4):
            rows = part[32 * y : 32 * y + 32]
            rows = [
                strips(8, [(rows[8 * m : 8 * m + 8], 0, 0, 96), (rows[24:32], 32 * m, 96, 32)]) for m in range(3)
            ]
            out[4 * y + (quarter - y) % 4, 96:120, :] = jnp.concatenate(rows, axis=0).astype(BF16)


def to_groups():
    return moves(128, lambda r, c: c == (((r >> 1) & 15) * 8 + (r >> 5) * 2 + (r & 1)))


def to_blocks():
    return moves(128, lambda r, c: c == (((r >> 1) & 3) * 32 + (r >> 3) * 2 + (r & 1)))


def attend(core, got, wo):
    sent = []
    for t in range(6):
        rows = [got[slot(core, i), 48 + 8 * t : 56 + 8 * t, :].astype(F32) for i in range(16)]
        sent.append(jnp.concatenate(rows, axis=0).astype(BF16))
    sent = dot(to_groups(), jnp.concatenate(sent, axis=1))
    low16 = lower_lanes(16)
    tiles = []
    for pair in range(2):
        groups = [[], [], []]
        for s in range(2):
            for half in range(2):
                even, odd = (got[8 * s + 4 * pair + 2 * o + half, 0:48, :].astype(F32) for o in range(2))
                e, o = even[0:16], odd[0:16]
                groups[0].append(even[16:48])
                groups[1] += [jnp.where(low16, swap(e), o), jnp.where(low16, e, swap(o))]
                groups[2].append(odd[16:48])
        tiles += [jnp.concatenate(g, axis=0) for g in groups]
    mixed = jnp.concatenate(tiles, axis=1).astype(BF16)
    return (sent + dot(mixed, wo[...])).astype(BF16)


def middle(core, got, wo, lifted):
    normed = layer_norm(attend(core, got, wo).astype(F32))
    result = (normed * normal_cdf(normed)).astype(BF16)
    for x in range(4):
        lifted[x] = result


def filtered(core, lifted, got, filters, gated, mine, theirs):
    rows = lifted[...].reshape(512, 768)
    taps = dot(rows, filters[...])
    place = lax.broadcasted_iota(jnp.int32, (512, 128), 0) & 31

    def from_below(tile):
        return jnp.where(place >= 4, pltpu.roll(tile, 4, 0), 0.0)

    def from_above(tile):
        return jnp.where(place < 28, pltpu.roll(tile, 508, 0), 0.0)

    hidden = from_below(taps[:, 0:128]) + taps[:, 128:256] + from_above(taps[:, 256:384])
    cdf = normal_cdf(hidden)
    gated[...] = (hidden * cdf).astype(BF16)
    pdf = jnp.exp(-0.5 * hidden * hidden) * (1.0 / math.sqrt(2.0 * math.pi))
    back = []
    came = [jnp.concatenate([got[slot(core, i), 96 + 8 * m : 104 + 8 * m, :].astype(F32) for i in range(16)], axis=0) for m in range(3)]
    for x in range(4):
        part = [(came[x], 0, 0, 96)] if x < 3 else [(came[m], 96, 32 * m, 32) for m in range(3)]
        back.append(dot(to_groups(), strips(128, part).astype(BF16)))
    slope = jnp.concatenate(back, axis=0) * (cdf + hidden * pdf)
    slope = slope.astype(BF16).astype(F32)
    below, above = from_above(slope), from_below(slope)
    packed = [
        strips(512, [(below, 0, 0, 96), (slope, 0, 96, 32)]),
        strips(512, [(slope, 32, 0, 64), (above, 0, 64, 64)]),
        strips(512, [(above, 64, 0, 32)]),
    ]
    packed = jnp.concatenate(packed, axis=1).astype(BF16)
    grad = dot(rows, packed, ((0,), (0,)))
    for d in range(16):
        halves = []
        for half in range(2):
            start = 48 * d + 24 * half
            part = grad[start : start + 24]
            last = strips(8, [(part[8 * m : 8 * m + 8, 256:384], 0, 32 * m, 32) for m in range(3)])
            halves.append(jnp.concatenate([part[:, 0:128], part[:, 128:256], last], axis=0))
        theirs[d] = jnp.where(core[0] == 0, halves[1], halves[0]).astype(BF16)
        mine[d] = jnp.where(core[0] == 0, halves[0], halves[1]).astype(BF16)


def rest(core, got, wo, gated, message):
    rows = dot(to_blocks(), attend(core, got, wo))
    gated = [dot(to_blocks(), gated[128 * x : 128 * x + 128, :]) for x in range(4)]
    gated = [strips(128, [(gated[m], 0, 0, 96), (gated[3], 32 * m, 96, 32)]) for m in range(3)]
    for i in range(16):
        block = slice(8 * i, 8 * i + 8)
        parts = [rows[block, 128 * t : 128 * t + 128] for t in range(6)] + [g[block] for g in gated]
        message[slot(core, i), 56:128, :] = jnp.concatenate(parts, axis=0).astype(BF16)


def joined(core, mine, came, begun, message):
    for d in range(16):
        message[slot(core, d), 0:56, :] = (mine[d].astype(F32) + came[d].astype(F32)).astype(BF16)


def summed(got, mix, grad, track):
    total = []
    for x in range(4):
        part = got[x, 0:56, :].astype(F32)
        for y in range(1, 4):
            part = part + got[4 * y + (x - y) % 4, 0:56, :].astype(F32)
        total.append(part)
    for near in range(4):
        half = 2 * (near % 2)
        grad[near] = jnp.concatenate(total[half : half + 2], axis=0).astype(BF16)
    natural = moves(128, lambda r, c: c == (((r >> 2) & 15) * 8 + (r >> 6) * 4 + (r & 3)))
    gated, weights = [], []
    for x in range(4):
        rows = []
        for y in range(4):
            part = got[4 * y + (x - y) % 4, 104:128, :].astype(F32)
            part = [part[8 * m : 8 * m + 8] for m in range(3)]
            rows += [strips(8, [(p, 0, 0, 96)]) for p in part]
            rows.append(strips(8, [(part[m], 96, 32 * m, 32) for m in range(3)]))
        gated.append(jnp.concatenate(rows, axis=0).astype(BF16))
        weights += [mix[128 * t + 32 * x : 128 * t + 32 * x + 32, :] for t in range(3)]
        weights.append(jnp.zeros((32, 768), BF16))
    attended = []
    for t in range(6):
        rows = [got[d, 56 + 8 * t : 64 + 8 * t, :].astype(F32) for d in range(16)]
        attended.append(jnp.concatenate(rows, axis=0).astype(BF16))
    gated = dot(natural, jnp.concatenate(gated, axis=1)).astype(BF16)
    attended = dot(natural, jnp.concatenate(attended, axis=1))
    track[...] = (attended + dot(gated, jnp.concatenate(weights, axis=0))).astype(BF16)


def summed_again(got, grad):
    total = got[0].astype(F32) + got[1].astype(F32) + got[2].astype(F32) + got[3].astype(F32)
    total = total.astype(BF16)
    for copy in range(grad.shape[0]):
        grad[copy] = total


def ordered(got, rows, target, track, grad, semaphores):
    copies = [
        pltpu.make_async_copy(rows, track, semaphores.at[0]),
        pltpu.make_async_copy(grad, target, semaphores.at[1]),
    ]
    copies[0].start()
    for core in range(2):
        sources = []
        for x in range(4):
            part = got[2 * (x // 2) + core, 56 * (x % 2) : 56 * (x % 2) + 56, :].astype(F32)
            last = part[48:56]
            last = jnp.concatenate([last, pltpu.roll(last, 96, 1), pltpu.roll(last, 64, 1)], axis=0)
            sources.append((part[0:24], part[24:48], last))
        for k in range(9):
            tile = strips(24, [(sources[x][k // 4], 32 * (k % 4), 32 * x, 32) for x in range(4)])
            grad[24 * core : 24 * core + 24, 128 * k : 128 * k + 128] = tile
    copies[1].start()
    for copy in copies:
        copy.wait()


def call(kernel, outs, *args, fetched=(), copies=0, in_hbm=(), out_hbm=(), limit=32, alias={}):
    hbm = pl.BlockSpec(memory_space=pl.ANY)
    return pl.pallas_call(
        kernel,
        out_shape=[jax.ShapeDtypeStruct(out[1:], F32) if out[0] == F32 else jax.ShapeDtypeStruct(out, BF16) for out in outs],
        in_specs=[
            SMEM if a.dtype == jnp.int32 else hbm if n in in_hbm else VMEM for n, a in enumerate(args)
        ],
        out_specs=[hbm if n in out_hbm else VMEM for n in range(len(outs))],
        scratch_shapes=[
            pltpu.VMEM(shape[1:], F32) if shape[0] == F32 else pltpu.VMEM(shape, BF16) for shape in fetched
        ]
        + ([pltpu.SemaphoreType.DMA((copies,))] if copies else []),
        input_output_aliases=alias,
        compiler_params=pltpu.CompilerParams(vmem_limit_bytes=limit * 1024 * 1024),
    )(*args)


def other_core(value):
    return lax.ppermute(value, "dp", [(source, source ^ 1) for source in range(32)])


def shards(
    features,
    query_weight,
    key_weight,
    value_weight,
    output_weight,
    dilated_weight,
    mixing_weight,
    cotangent,
):
    core = lax.axis_index("dp") % 2
    flag = core.astype(jnp.int32).reshape(1)
    rows, slope = features.reshape(128, 768), cotangent.reshape(128, 768)
    (message,) = call(
        front,
        [(16, 256, 128)],
        flag,
        rows,
        dilated_weight,
        query_weight,
        key_weight,
        value_weight,
        fetched=((128, 768), (48, 1152), (768, 256), (768, 256), (768, 768)),
        copies=8,
        in_hbm=(1, 2, 3, 4, 5),
        limit=56,
    )
    got = lax.all_to_all(message, ("dp", "ctx"), 0, 0, axis_index_groups=CTX)
    mixed, filters = call(attention, [(16, 120, 128), (768, 384)], flag, got, rows, slope, mixing_weight)
    got = lax.all_to_all(mixed, ("dp", "ctx"), 0, 0, axis_index_groups=CTX)
    (lifted,) = call(middle, [(4, 128, 768)], flag, got, output_weight)
    lifted = lax.all_to_all(lifted, ("dp", "ctx"), 0, 0, axis_index_groups=ACROSS)
    gated, mine, theirs = call(
        filtered, [(512, 128), (16, 56, 128), (16, 56, 128)], flag, lifted, got, filters
    )
    came = other_core(theirs)
    (message,) = call(rest, [(16, 128, 128)], flag, got, output_weight, gated)
    (message,) = call(joined, [(16, 128, 128)], flag, mine, came, message, alias={3: 0})
    got = lax.all_to_all(message, ("dp", "ctx"), 0, 0, axis_index_groups=CTX)
    grad, track = call(summed, [(4, 112, 128), (128, 768)], got, mixing_weight)
    got = lax.all_to_all(grad, "dp", 0, 0, axis_index_groups=NEAR)
    (grad,) = call(summed_again, [(4, 112, 128)], got)
    got = lax.all_to_all(grad, "dp", 0, 0, axis_index_groups=FAR)
    (grad,) = call(summed_again, [(4, 112, 128)], got)
    got = lax.all_to_all(grad, "dp", 0, 0, axis_index_groups=CLOSE)
    dilated_grad, track = call(
        ordered, [(F32, 48, 1152), (128, 768)], got, track, fetched=((F32, 48, 1152),), copies=2, out_hbm=(0, 1)
    )
    return (track.reshape(2, 64, 768), dilated_grad)


def solution(mesh):
    return jax.shard_map(
        shards,
        mesh=mesh,
        in_specs=(
            P("dp", "ctx", None),
            P(),
            P(),
            P(),
            P(),
            P("ctx", None),
            P(),
            P("dp", "ctx", None),
        ),
        out_specs=(P("dp", "ctx", None), P("ctx", None)),
        check_vma=False,
    )
```
